128 devices in a mesh: rep: 16 (over y, x_hi, core), tp: 8 (over z, x_lo).
Axes of the slice: x: 4 (x_hi: 2, x_lo: 2; x = x_hi * 2 + x_lo), y: 4, z: 4, core: 2. Of those that a mesh axis runs over, the one named last changes fastest.
Arguments:
- latent_cache: bfloat16 [16, 8192, 576], P('rep', 'tp'), may hold values from -8 to 8
- query_nope: bfloat16 [384, 16384], P('rep', 'tp'), may hold values from -6 to 6
- query_rope: bfloat16 [384, 8192], P('rep', 'tp'), may hold values from -7 to 7
- new_latent: bfloat16 [384, 576], P('rep'), may hold values from -8 to 8
- key_up: bfloat16 [128, 128, 512], P('tp'), may hold values from -0.5 to 0.5
- value_up: bfloat16 [128, 512, 128], P('tp'), may hold values from -0.75 to 0.75
- prompt_owner: int32 [16], replicated, may hold values from 0 to 15, each once
- prompt_length: int32 [16], replicated, may hold values from 1024 to 8192, as said below
- sample_prompt: int32 [384, 1], P('rep'), may hold values from 0 to 15; in each aligned block of 24 rows (0 to 23, 24 to 47, ...) at most 3 rows name the same one
Outputs:
- head_output: bfloat16 [384, 16384], P('rep', 'tp')
The draws below stay inside these ranges and needn't reach their ends.
Inputs may be any that keep to these rules, and one draw needn't show every extreme that they name: `sample_prompt`: the rows of one replica group, 24 of them, name no prompt more than 3 times, a bound that some block reaches. `prompt_length`: one prompt has all 8192 positions live and one has 1024.
All inputs are finite; a program needn't handle non-finite values.
Results may differ from the reference program's by a relative error of at most 0.0073.
Values may be sent and summed in bfloat16 or wider, within the bound.
A program may use at most 128 MiB of HBM per device.

```python
import math
import jax
import jax.numpy as jnp
import numpy as np
from jax import lax

H = 128
D_NOPE = 128
D_ROPE = 64
D_LAT = 512
D_V = 128
D_KV = 576
SPG = 24
CAP = 3
LEN = 8192
PROMPTS = 16
SAMPLES = 384


def draw_latent_cache(key, part):
    key = jax.random.fold_in(key, 3)
    shape = (PROMPTS, LEN, D_KV)
    values = jnp.clip(1.4 * jax.random.normal(key, shape, jnp.float32), -8.0, 8.0)
    return values.astype(jnp.bfloat16)


def draw_query_rope(key, part):
    key = jax.random.fold_in(key, 5)
    shape = (SAMPLES, H, D_ROPE)
    values = jnp.clip(jax.random.normal(key, shape, jnp.float32), -6.0, 6.0)
    return values.reshape(SAMPLES, H * D_ROPE).astype(jnp.bfloat16)


def draw_prompt_length(key, part):
    key = jax.random.fold_in(key, 7)
    lengths = jax.random.randint(key, (PROMPTS,), LEN // 8, LEN + 1)
    ordering = jax.random.permutation(jax.random.fold_in(key, 1), PROMPTS)
    lengths = lengths.at[ordering[0]].set(LEN)
    lengths = lengths.at[ordering[1]].set(LEN // 8)
    return lengths.astype(jnp.int32)


def block_scale(stream_key, shape, split, least, high):
    gain = 1.0
    for dim, blocks in split:
        draws = jax.random.uniform(jax.random.fold_in(jax.random.fold_in(stream_key, 6), dim), (blocks,), jnp.float32, least / len(split), high / len(split))
        gain = gain * jnp.repeat(jnp.exp(draws), shape[dim] // blocks).reshape((-1,) + (1,) * (len(shape) - 1 - dim))
    return gain


def shared_out(rng, own, number, rows, count, top, most, lean):
    order = jax.random.permutation(rng, count)
    crowded, usual = portions_of(count, rows * top, most, lean, True), portions_of(count, rows * top, most, lean, False)
    places = jnp.arange(count)

    def named(sizes, rotation):
        used = int((sizes > 0).sum())
        fixed = max(1, used // 4)
        shifted = fixed + (places - fixed + rotation * (used - fixed)) % max(1, count - fixed)
        return jnp.zeros((count,), jnp.int32).at[order[jnp.where(places < fixed, places, shifted)]].set(jnp.asarray(sizes, jnp.int32))

    sizes = jnp.where(number % 4 == 0, named(crowded, number // 4), named(usual, number - number // 4 - 1))
    mixed = jax.random.permutation(jax.random.fold_in(own, 3), count)
    giver, receiver = mixed[0:count // 2 * 2:2], mixed[1:count // 2 * 2:2]
    slack = jnp.minimum(sizes[giver] - 1, most - sizes[receiver]) // 2
    slack = jnp.where((giver == order[0]) | (receiver == order[0]) | (sizes[receiver] == 0), 0, jnp.maximum(slack, 0))
    shifted = jax.random.randint(jax.random.fold_in(own, 4), (count // 2,), 0, 1 << 20) % (slack + 1)
    sizes = sizes.at[giver].add(-shifted).at[receiver].add(shifted)
    labels = jnp.searchsorted(jnp.cumsum(sizes), jnp.arange(rows * top), side="right").astype(jnp.int32)
    table = labels.reshape(top, rows).T
    table = table[jax.random.permutation(jax.random.fold_in(own, 1), rows)]
    rotation = jax.random.randint(jax.random.fold_in(own, 2), (rows, 1), 0, top)
    return jnp.take_along_axis(table, (jnp.arange(top)[None, :] + rotation) % top, axis=1)


def portions_of(amount, total, most, slope, full):
    loads = [(1 << 20) // math.isqrt(grade ** slope) + 1 for grade in range(1, amount + 1)]
    largest = most if full else min(most, max(-(-total // amount), total * loads[0] // sum(loads)))
    least = 1 if total - largest >= amount - 1 else 0
    given, spare = [largest] + [least] * (amount - 1), total - largest - least * (amount - 1)
    while spare > 0:
        free = [i for i in range(1, amount) if given[i] < largest] or [i for i in range(1, amount) if given[i] < most]
        whole, left = sum([loads[i] for i in free]), spare
        for i in free:
            addition = min(most - given[i], max(1, left * loads[i] // whole), spare)
            given[i] = given[i] + addition
            spare = spare - addition
    return np.array(given)


def noise(stream_key, shape, deviation, reach, cuts=(), kind=jnp.bfloat16):
    entries = jax.random.normal(stream_key, shape, jnp.float32) * deviation
    if len(cuts) > 0:
        entries = block_scale(stream_key, shape, cuts, -0.22, 0.18) * entries
    return jnp.clip(entries, min=-reach, max=reach).astype(kind)


def setup_inputs(seed: int = 0) -> dict:
    key_of = jax.random.split(jax.random.key(seed), 10)
    latent_cache = draw_latent_cache(jax.random.fold_in(key_of[9], 71), 0)
    query_nope = noise(key_of[1], (SAMPLES, H * D_NOPE), 1.0, 6.0, ((0, 16), (1, 8)))
    query_rope = draw_query_rope(jax.random.fold_in(key_of[9], 71), 0)
    new_latent = noise(key_of[3], (SAMPLES, D_KV), 1.4, 8.0, ((0, 16),))
    key_up = noise(key_of[4], (H, D_NOPE, D_LAT), D_NOPE ** -0.5, 0.5, ((0, 8),))
    value_up = noise(key_of[5], (H, D_LAT, D_V), (D_LAT // 8) ** -0.5, 0.75, ((0, 8),))
    prompt_owner = jax.random.permutation(key_of[6], PROMPTS).astype(jnp.int32)
    prompt_length = draw_prompt_length(jax.random.fold_in(key_of[9], 71), 0)
    sample_prompt_keys = jax.random.split(jax.random.fold_in(key_of[8], 1), SAMPLES // SPG)
    sample_prompt_turns = jax.random.permutation(jax.random.fold_in(key_of[8], 3), SAMPLES // SPG)
    sample_prompt = jax.vmap(lambda own, number: shared_out(jax.random.fold_in(key_of[8], 2), own, number, SPG, PROMPTS, 1, CAP, 2))(sample_prompt_keys, sample_prompt_turns).reshape((SAMPLES, 1))
    return {"latent_cache": latent_cache, "query_nope": query_nope, "query_rope": query_rope, "new_latent": new_latent, "key_up": key_up, "value_up": value_up, "prompt_owner": prompt_owner, "prompt_length": prompt_length, "sample_prompt": sample_prompt}


big_negative = -1.0e30


def reference(latent_cache, query_nope, query_rope, new_latent, key_up, value_up, prompt_owner, prompt_length, sample_prompt):
    samples = query_nope.shape[0]
    head_count, nope_width, latent_width = key_up.shape
    nope_part = query_nope.reshape(samples, head_count, nope_width).astype(jnp.float32)
    rope_part = query_rope.reshape(samples, head_count, -1).astype(jnp.float32)
    latent_query = jnp.einsum("shn,hnl->shl", nope_part, key_up.astype(jnp.float32))
    scaling = (nope_width + rope_part.shape[2]) ** -0.5
    absorbed = (jnp.concatenate([latent_query, rope_part], axis=2) * scaling).astype(jnp.bfloat16)
    position = jnp.arange(latent_cache.shape[1], dtype=jnp.int32)

    def one_sample(sample_index):
        prompt_id = sample_prompt[sample_index, 0]
        slot_id = prompt_owner[prompt_id].astype(jnp.int32)
        prefix_keys = lax.dynamic_index_in_dim(latent_cache, slot_id, 0, keepdims=False)
        length = prompt_length[prompt_id]
        query_rows = lax.dynamic_index_in_dim(absorbed, sample_index, 0, keepdims=False)
        fresh_latent = lax.dynamic_index_in_dim(new_latent, sample_index, 0, keepdims=False)
        scores = jnp.dot(query_rows, prefix_keys.T, preferred_element_type=jnp.float32)
        scores = jnp.where(position[None, :] < length, scores, big_negative)
        own_score = jnp.dot(query_rows, fresh_latent, preferred_element_type=jnp.float32)
        row_top = jnp.maximum(jnp.max(scores, axis=1), own_score)
        weights = jnp.exp(scores - row_top[:, None])
        own_weight = jnp.exp(own_score - row_top)
        totals = jnp.sum(weights, axis=1) + own_weight
        numerator = jnp.dot(weights.astype(jnp.bfloat16), prefix_keys[:, :latent_width], preferred_element_type=jnp.float32)
        numerator = numerator + own_weight[:, None] * fresh_latent[None, :latent_width].astype(jnp.float32)
        latent_out = (numerator / totals[:, None]).astype(jnp.bfloat16)
        values = jnp.einsum("hl,hlv->hv", latent_out.astype(jnp.float32), value_up.astype(jnp.float32))
        return values.astype(jnp.bfloat16).reshape(-1)

    return lax.map(one_sample, jnp.arange(samples, dtype=jnp.int32))
```

```python
import functools

import jax
import jax.numpy as jnp
from jax import lax
from jax.experimental import pallas as pl
from jax.experimental.pallas import tpu as pltpu
from jax.sharding import PartitionSpec as P

MESH = pl.DeviceIdType.MESH
NEG = -1e30
F32, BF16 = jnp.float32, jnp.bfloat16

S, HL, SLOTS, CAP = 24, 16, 16, 3
PL = SLOTS * CAP
ROWS = PL * HL
LAT, ROPE, NOPE, DV = 512, 64, 128, 128
QW = LAT + 2 * ROPE
SHARD, CH = 1024, 512
PK = CH + CH * ROPE // LAT
RB = 256


def dot(a, b):
    return jnp.dot(a, b, preferred_element_type=F32)


def dot_nt(a, b):
    return lax.dot_general(a, b, (((1,), (1,)), ((), ())), preferred_element_type=F32)


def block(i):
    return pl.ds(pl.multiple_of(i * (CAP * HL), 16), CAP * HL)


def iota(shape, dim):
    return lax.broadcasted_iota(jnp.int32, shape, dim)


def kernel(
    latent, nope_h, rope_h, new_h, ku_h, vu_h, owner, length, labels, out,
    nope, rope, new, ku, vu, rtmp, kv, stage, qsend, q, qhi, mtop, tot, acc, osend, orecv,
    lsem, qss, qrs, kss, krs, vss, vrs, oss, ors,
):
    r, t = lax.axis_index("rep"), lax.axis_index("tp")
    y, xh, c, z, xl = r // 4, (r // 2) % 2, r % 2, t // 2, t % 2
    role_a = c == xl

    def dev(yy, xx, zz, cc):
        return ((yy * 2 + xx // 2) * 2 + cc, zz * 2 + xx % 2)

    x = xh * 2 + xl
    zp, zm = dev(y, x, (z + 1) % 4, c), dev(y, x, (z + 3) % 4, c)
    sib = dev(y, x, z, 1 - c)
    partner = dev(y, xh * 2 + 1 - xl, z, 1 - c)
    slot = (y * 2 + xh) * 2 + xl

    base = jnp.where(role_a, 0, 16)
    loads = [
        pltpu.make_async_copy(nope_h, nope, lsem.at[0]),
        pltpu.make_async_copy(rope_h, rope, lsem.at[1]),
        pltpu.make_async_copy(new_h, new, lsem.at[2]),
        pltpu.make_async_copy(ku_h, ku, lsem.at[3]),
        pltpu.make_async_copy(latent.at[0, :, pl.ds(LAT, ROPE)], rtmp, lsem.at[4]),
        pltpu.make_async_copy(latent.at[0, pl.ds(0, CH), pl.ds(0, LAT)], kv.at[base, pl.ds(0, CH)], lsem.at[5]),
        pltpu.make_async_copy(latent.at[0, pl.ds(CH, CH), pl.ds(0, LAT)], kv.at[base + 1, pl.ds(0, CH)], lsem.at[6]),
    ]
    for load in loads:
        load.start()
    vload = pltpu.make_async_copy(vu_h, vu, lsem.at[7])
    pl.when(role_a)(vload.start)

    barrier = pltpu.get_barrier_semaphore()

    def greet_core(i, _):
        @pl.when(jnp.logical_not(jnp.logical_and(role_a, i == y * 4 + x)))
        def _():
            pl.semaphore_signal(barrier, inc=1, device_id=dev(i // 4, i % 4, z, xl), device_id_type=MESH)
        return 0

    def greet_col(i, _):
        pl.semaphore_signal(barrier, inc=1, device_id=dev(i // 2, (i % 2) * 2 + c, z, 1 - xl), device_id_type=MESH)
        return 0

    for d in (zp, zm):
        pl.semaphore_signal(barrier, inc=1, device_id=d, device_id_type=MESH)
    lax.fori_loop(0, 16, greet_core, 0)
    lax.fori_loop(0, 8, greet_col, 0)

    for i in (4, 5, 6):
        loads[i].wait()
    spread = iota((ROPE, 2 * ROPE), 0) - iota((ROPE, 2 * ROPE), 1)
    lo_e, hi_e = (spread == 0).astype(BF16), (spread == -ROPE).astype(BF16)
    half = CH // 2
    for k in range(2):
        packed = dot(rtmp[pl.ds(k * CH, half), :], lo_e) + dot(rtmp[pl.ds(k * CH + half, half), :], hi_e)
        packed = packed.astype(BF16)
        for j in range(4):
            kv[base + k, pl.ds(CH, PK - CH), pl.ds(128 * j, 128)] = packed[64 * j : 64 * j + 64]

    lab = labels[...]
    sub, lane = iota((S, S), 0), iota((S, S), 1)
    lab_row = jnp.sum(jnp.where(sub == lane, lab.astype(F32), 0.0), axis=0, keepdims=True).astype(jnp.int32)
    same = lab == lab_row
    rank_row = jnp.sum(jnp.where(same & (sub < lane), 1.0, 0.0), axis=0, keepdims=True).astype(jnp.int32)
    rank_col = jnp.sum(jnp.where(same & (lane < sub), 1.0, 0.0), axis=1, keepdims=True).astype(jnp.int32)
    slot_row, slot_col = jnp.zeros_like(lab_row), jnp.zeros_like(lab)
    live = jnp.int32(0)
    for p in range(SLOTS):
        own = owner[p]
        slot_row = jnp.where(lab_row == p, own, slot_row)
        slot_col = jnp.where(lab == p, own, slot_col)
        live = live + jnp.where(own == slot, length[p], 0)
    place = (iota((PL, S), 0) == slot_row * CAP + rank_row).astype(BF16)
    unplace = (iota((S, PL), 1) == slot_col * CAP + rank_col).astype(BF16)

    for i in (0, 1, 2, 3):
        loads[i].wait()
    scale = (NOPE + ROPE) ** -0.5
    nope_s = dot(place, nope[...]).astype(BF16)
    rope_s = dot(place, rope[...]) * scale
    new_s = dot(place, new[...])
    new_s = jnp.concatenate([new_s[:, :LAT], jnp.concatenate([new_s[:, LAT:], jnp.zeros((PL, ROPE), F32)], axis=1)], axis=1)
    low = iota((PL, 2 * ROPE), 1) < ROPE
    for h in range(HL):
        rows = pl.ds(h, PL, stride=HL)
        lat_q = dot(nope_s[:, NOPE * h : NOPE * (h + 1)], ku[h]) * scale
        for j in range(4):
            stage[j, rows, :] = lat_q[:, 128 * j : 128 * j + 128]
        b = 128 * (h // 2)
        mine = rope_s[:, b : b + 128]
        if h % 2:
            mine = pltpu.roll(mine, ROPE, 1)
        if h < 9:
            piece = new_s[:, b : b + 128]
            if h % 2 == 0:
                piece = pltpu.roll(piece, ROPE, 1)
        else:
            piece = jnp.zeros_like(mine)
        stage[4, rows, :] = jnp.where(low, mine, piece)
    for j in range(5):
        qsend[:, pl.ds(128 * j, 128)] = stage[j].astype(BF16)

    def q_copy(s, d):
        return pltpu.make_async_remote_copy(
            src_ref=qsend.at[block(s)], dst_ref=q.at[block(r)], send_sem=qss.at[s], recv_sem=qrs.at[r], device_id=d, device_id_type=MESH
        )

    def q_dev(s):
        return dev(s // 4, ((s // 2) % 2) * 2 + s % 2, z, xl)

    own_q = pltpu.make_async_copy(qsend.at[block(r)], q.at[block(r)], qrs.at[r])

    def kv_copy(src, dst, sem, d):
        return pltpu.make_async_remote_copy(
            src_ref=kv.at[src], dst_ref=kv.at[dst], send_sem=kss.at[sem], recv_sem=krs.at[dst], device_id=d, device_id_type=MESH
        )

    o = jnp.where(role_a, 0, 8)

    def ring_own(k):
        return [kv_copy(o + k, o + 2 + k, k, zp), kv_copy(o + k, o + 4 + k, 2 + k, zm), kv_copy(o + k, o + k, 8 + k, sib)]

    def ring_pass(k):
        out_ = [kv_copy(o + k, o + k, 8 + k, sib)]
        if k == 2:
            out_.insert(0, kv_copy(o + 2, o + 6, 4, zp))
        if k == 5:
            out_.insert(0, kv_copy(o + 5, o + 7, 5, zm))
        return out_

    def arrived(k):
        kv_copy(k, k, 0, sib).wait_recv()

    def ring_step(k):
        arrived(o + k)
        for cp in ring_pass(k):
            cp.start()

    cross = [kv_copy(16 + k, 8 + k, 16 + k, partner) for k in range(2)]

    pl.semaphore_wait(barrier, jnp.where(role_a, 25, 26))

    @pl.when(role_a)
    def _():
        for k in range(2):
            for cp in ring_own(k):
                cp.start()

    def q_send(i, _):
        s = (slot + i) % SLOTS

        @pl.when(jnp.logical_and(role_a, i == 0))
        def _():
            own_q.start()

        @pl.when(jnp.logical_not(jnp.logical_and(role_a, i == 0)))
        def _():
            q_copy(s, q_dev(s)).start()
        return 0

    lax.fori_loop(0, SLOTS, q_send, 0)

    @pl.when(jnp.logical_not(role_a))
    def _():
        for cp in cross:
            cp.start()

    @pl.when(role_a)
    def _():
        for k in (2, 4, 3, 5):
            ring_step(k)

    @pl.when(jnp.logical_not(role_a))
    def _():
        arrived(8)
        for cp in ring_own(0):
            cp.start()

    def q_wait(i, _):
        g = (r + i) % SLOTS

        @pl.when(jnp.logical_and(role_a, i == 0))
        def _():
            own_q.wait()

        @pl.when(jnp.logical_not(jnp.logical_and(role_a, i == 0)))
        def _():
            pltpu.make_async_remote_copy(
                src_ref=qsend.at[block(0)], dst_ref=q.at[block(g)], send_sem=qss.at[0], recv_sem=qrs.at[g], device_id=sib, device_id_type=MESH
            ).wait_recv()
        return 0

    lax.fori_loop(0, SLOTS, q_wait, 0)

    halves = [
        pltpu.make_async_remote_copy(
            src_ref=vu_h.at[pl.ds(8 * k, 8)], dst_ref=vu.at[pl.ds(8 * k, 8)], send_sem=vss.at[k], recv_sem=vrs.at[k],
            device_id=dev(y, (xh if k == 0 else 1 - xh) * 2 + 1 - xl, z, c), device_id_type=MESH,
        )
        for k in range(2)
    ]

    @pl.when(role_a)
    def _():
        for cp in halves:
            cp.start()

    q3 = q[...]
    tail = q3[:, LAT:].astype(F32)
    wide_low = iota((ROWS, 2 * ROPE), 1) < ROPE
    stage[0] = tail
    tail = jnp.where(wide_low, tail, 0.0)
    qhi[...] = pltpu.roll(tail, ROPE, 1).astype(BF16)
    pieces = [stage[0, pl.ds(k, PL, stride=HL), :] for k in range(9)]
    new_p = []
    for k in range(5):
        left = pltpu.roll(pieces[2 * k], ROPE, 1)
        new_p.append(jnp.where(low, left, pieces[2 * k + 1] if k < 4 else 0.0))
    new_p = jnp.concatenate(new_p, axis=1).astype(BF16)
    by_row = (iota((ROWS, PL), 0) // HL == iota((ROWS, PL), 1)).astype(BF16)
    own_keys = dot(by_row, new_p)
    own_score = jnp.sum(q3[:, :LAT].astype(F32) * own_keys[:, :LAT], axis=1, keepdims=True)
    own_score = own_score + jnp.sum(tail * own_keys[:, LAT:], axis=1, keepdims=True)
    for j in range(4):
        acc[j] = own_keys[:, 128 * j : 128 * j + 128]
    mtop[...] = jnp.broadcast_to(own_score, mtop.shape)
    tot[...] = jnp.ones_like(tot)
    q[:, pl.ds(LAT, 2 * ROPE)] = tail.astype(BF16)

    def attend(ci):
        place_z = (ci % 8) // 2
        zz = (z + jnp.where(place_z == 1, 3, jnp.where(place_z == 2, 1, jnp.where(place_z == 3, 2, 0)))) % 4
        first = (zz * 2 + jnp.where(ci < 8, xl, 1 - xl)) * SHARD + (ci % 2) * CH
        keys = kv[ci, pl.ds(0, CH), :]
        rot = kv[ci, pl.ds(CH, PK - CH), :]
        rot = jnp.concatenate([rot[:, 128 * j : 128 * j + 128] for j in range(4)], axis=0)
        k_lo = jnp.concatenate([keys[:half], rot], axis=1)
        k_hi = jnp.concatenate([keys[half:], rot], axis=1)
        bias = jnp.where(first + iota((1, CH), 1) < live, 0.0, NEG)
        for b in range(ROWS // RB):
            rs = pl.ds(b * RB, RB)
            s_lo = dot_nt(q[rs, :], k_lo)
            s_hi = dot_nt(jnp.concatenate([q[rs, pl.ds(0, LAT)], qhi[rs, :]], axis=1), k_hi)
            s = jnp.concatenate([s_lo, s_hi], axis=1) + bias
            top = mtop[rs, pl.ds(0, 1)]
            new_top = jnp.maximum(top, jnp.max(s, axis=1, keepdims=True))
            shrink = jnp.exp(top - new_top)
            w = jnp.exp(s - new_top)
            tot[rs, :] = jnp.broadcast_to(tot[rs, pl.ds(0, 1)] * shrink + jnp.sum(w, axis=1, keepdims=True), (RB, 128))
            mtop[rs, :] = jnp.broadcast_to(new_top, (RB, 128))
            new = dot(w.astype(BF16), keys)
            for j in range(4):
                acc[j, rs, :] = acc[j, rs, :] * shrink + new[:, 128 * j : 128 * j + 128]

    def step(i, _):
        ci = i + (i % 8 == 3).astype(jnp.int32) - (i % 8 == 4).astype(jnp.int32)

        @pl.when(role_a)
        def _():
            for at, k in ((5, 6), (6, 7)):
                pl.when(i == at)(functools.partial(ring_step, k))
            pl.when(i >= 8)(lambda: arrived(ci))

        @pl.when(jnp.logical_not(role_a))
        def _():
            pl.when(i < 8)(lambda: arrived(ci))

            @pl.when(i == 2)
            def _():
                arrived(9)
                for cp in ring_own(1):
                    cp.start()

            for at, k in ((9, 2), (10, 4), (11, 3), (12, 5), (13, 6), (14, 7)):
                pl.when(i == at)(functools.partial(ring_step, k))

        attend(ci)
        return 0

    lax.fori_loop(0, 16, step, 0)

    @pl.when(role_a)
    def _():
        vload.wait()

    @pl.when(jnp.logical_not(role_a))
    def _():
        for cp in halves:
            cp.wait_recv()

    for h in range(HL):
        rows = pl.ds(h, PL, stride=HL)
        total = tot[rows, :]
        mean = jnp.concatenate([acc[j, rows, :] / total for j in range(4)], axis=1).astype(BF16)
        stage[0, rows, :] = dot(mean, vu[h])
    osend[...] = stage[0].astype(BF16)

    def o_copy(g):
        return pltpu.make_async_remote_copy(
            src_ref=osend.at[block(g)], dst_ref=orecv.at[block(slot)], send_sem=oss.at[g], recv_sem=ors.at[slot],
            device_id=(g, z * 2 + c), device_id_type=MESH,
        )

    own_o = pltpu.make_async_copy(osend.at[block(r)], orecv.at[block(r)], ors.at[r])

    def o_send(i, _):
        g = (r + i) % SLOTS
        kept = jnp.logical_and(role_a, i == 0)
        pl.when(kept)(own_o.start)
        pl.when(jnp.logical_not(kept))(lambda: o_copy(g).start())
        return 0

    lax.fori_loop(0, SLOTS, o_send, 0)

    @pl.when(role_a)
    def _():
        for cp in halves:
            cp.wait_send()

    @pl.when(jnp.logical_not(role_a))
    def _():
        for cp in cross:
            cp.wait_send()

    for k in range(2):
        for cp in ring_own(k):
            cp.wait_send()
    for k in range(2, 8):
        for cp in ring_pass(k):
            cp.wait_send()

    def all_wait(i, _):
        s = (slot + i) % SLOTS
        g = (r + i) % SLOTS
        kept = jnp.logical_and(role_a, i == 0)

        @pl.when(kept)
        def _():
            own_o.wait()

        @pl.when(jnp.logical_not(kept))
        def _():
            q_copy(s, sib).wait_send()
            o_copy(g).wait_send()
            pltpu.make_async_remote_copy(
                src_ref=osend.at[block(0)], dst_ref=orecv.at[block(s)], send_sem=oss.at[0], recv_sem=ors.at[s],
                device_id=sib, device_id_type=MESH,
            ).wait_recv()
        return 0

    lax.fori_loop(0, SLOTS, all_wait, 0)
    stage[0] = orecv[...].astype(F32)
    for h in range(HL):
        picked = stage[0, pl.ds(h, PL, stride=HL), :].astype(BF16)
        out[:, pl.ds(DV * h, DV)] = dot(unplace, picked).astype(BF16)


def shards(latent_cache, query_nope, query_rope, new_latent, key_up, value_up, prompt_owner, prompt_length, sample_prompt):
    hbm, smem, vmem = (pl.BlockSpec(memory_space=m) for m in (pl.ANY, pltpu.SMEM, pltpu.VMEM))
    dma = pltpu.SemaphoreType.DMA
    return pl.pallas_call(
        kernel,
        out_shape=jax.ShapeDtypeStruct(query_nope.shape, BF16),
        in_specs=[hbm] * 6 + [smem] * 2 + [vmem],
        out_specs=vmem,
        scratch_shapes=[
            pltpu.VMEM(query_nope.shape, BF16),
            pltpu.VMEM(query_rope.shape, BF16),
            pltpu.VMEM(new_latent.shape, BF16),
            pltpu.VMEM(key_up.shape, BF16),
            pltpu.VMEM(value_up.shape, BF16),
            pltpu.VMEM((SHARD, ROPE), BF16),
            pltpu.VMEM((18, PK, LAT), BF16),
            pltpu.VMEM((5, ROWS, 128), F32),
            pltpu.VMEM((ROWS, QW), BF16),
            pltpu.VMEM((ROWS, QW), BF16),
            pltpu.VMEM((ROWS, 2 * ROPE), BF16),
            pltpu.VMEM((ROWS, 128), F32),
            pltpu.VMEM((ROWS, 128), F32),
            pltpu.VMEM((4, ROWS, 128), F32),
            pltpu.VMEM((ROWS, DV), BF16),
            pltpu.VMEM((ROWS, DV), BF16),
            dma((8,)), dma((SLOTS,)), dma((SLOTS,)), dma((18,)), dma((16,)),
            dma((2,)), dma((2,)), dma((SLOTS,)), dma((SLOTS,)),
        ],
        compiler_params=pltpu.CompilerParams(collective_id=0, has_side_effects=True, vmem_limit_bytes=56 << 20),
        cost_estimate=pl.CostEstimate(flops=16 << 30, bytes_accessed=8 << 20, transcendentals=8 << 20),
    )(latent_cache, query_nope, query_rope, new_latent, key_up, value_up, prompt_owner, prompt_length, sample_prompt)


def solution(mesh):
    return jax.shard_map(
        shards,
        mesh=mesh,
        in_specs=(
            P("rep", "tp", None),
            P("rep", "tp"),
            P("rep", "tp"),
            P("rep", None),
            P("tp", None, None),
            P("tp", None, None),
            P(),
            P(),
            P("rep", None),
        ),
        out_specs=P("rep", "tp"),
        check_vma=False,
    )
```

```python
import functools

import jax
import jax.numpy as jnp
from jax import lax
from jax.experimental import pallas as pl
from jax.experimental.pallas import tpu as pltpu
from jax.sharding import PartitionSpec as P

MESH = pl.DeviceIdType.MESH
NEG = -1e30
F32, BF16 = jnp.float32, jnp.bfloat16

S, HL, SLOTS, CAP = 24, 16, 16, 3
PL = SLOTS * CAP
ROWS = PL * HL
LAT, ROPE, NOPE, DV = 512, 64, 128, 128
QW = LAT + 2 * ROPE
SHARD, SUB = 1024, 256
CH = 2 * SUB
KW = LAT + ROPE
RB = 256


def dot(a, b):
    return jnp.dot(a, b, preferred_element_type=F32)


def dot_nt(a, b):
    return lax.dot_general(a, b, (((1,), (1,)), ((), ())), preferred_element_type=F32)


def block(i):
    return pl.ds(pl.multiple_of(i * (CAP * HL), 16), CAP * HL)


def iota(shape, dim):
    return lax.broadcasted_iota(jnp.int32, shape, dim)


def kernel(
    latent, nope_h, rope_h, new_h, ku_h, vu_h, owner, length, labels, out,
    nope, rope, new, ku, vu, kv, stage, qsend, q, mtop, tot, acc, osend, orecv,
    lsem, qss, qrs, kss, krs, vss, vrs, oss, ors,
):
    r, t = lax.axis_index("rep"), lax.axis_index("tp")
    y, xh, c, z, xl = r // 4, (r // 2) % 2, r % 2, t // 2, t % 2
    role_a = c == xl

    def dev(yy, xx, zz, cc):
        return ((yy * 2 + xx // 2) * 2 + cc, zz * 2 + xx % 2)

    x = xh * 2 + xl
    zp, zm = dev(y, x, (z + 1) % 4, c), dev(y, x, (z + 3) % 4, c)
    sib = dev(y, x, z, 1 - c)
    partner = dev(y, xh * 2 + 1 - xl, z, 1 - c)
    slot = (y * 2 + xh) * 2 + xl

    base = jnp.where(role_a, 0, 32)
    loads = [
        pltpu.make_async_copy(nope_h, nope, lsem.at[0]),
        pltpu.make_async_copy(rope_h, rope, lsem.at[1]),
        pltpu.make_async_copy(new_h, new, lsem.at[2]),
        pltpu.make_async_copy(ku_h, ku, lsem.at[3]),
    ] + [pltpu.make_async_copy(latent.at[0, :, pl.ds(u * SUB, SUB)], kv.at[base + u], lsem.at[4 + u]) for u in range(4)]
    for load in loads:
        load.start()
    vload = pltpu.make_async_copy(vu_h, vu, lsem.at[8])
    pl.when(role_a)(vload.start)

    barrier = pltpu.get_barrier_semaphore()

    def greet_core(i, _):
        @pl.when(jnp.logical_not(jnp.logical_and(role_a, i == y * 4 + x)))
        def _():
            pl.semaphore_signal(barrier, inc=1, device_id=dev(i // 4, i % 4, z, xl), device_id_type=MESH)
        return 0

    def greet_col(i, _):
        pl.semaphore_signal(barrier, inc=1, device_id=dev(i // 2, (i % 2) * 2 + c, z, 1 - xl), device_id_type=MESH)
        return 0

    for d in (zp, zm):
        pl.semaphore_signal(barrier, inc=1, device_id=d, device_id_type=MESH)
    lax.fori_loop(0, 16, greet_core, 0)
    lax.fori_loop(0, 8, greet_col, 0)

    lab_row = labels[...]
    sub, lane = iota((S, S), 0), iota((S, S), 1)
    lab = jnp.sum(jnp.where(sub == lane, lab_row.astype(F32), 0.0), axis=1, keepdims=True).astype(jnp.int32)
    same = lab == lab_row
    rank_row = jnp.sum(jnp.where(same & (sub < lane), 1.0, 0.0), axis=0, keepdims=True).astype(jnp.int32)
    rank_col = jnp.sum(jnp.where(same & (lane < sub), 1.0, 0.0), axis=1, keepdims=True).astype(jnp.int32)
    slot_row, slot_col = jnp.zeros_like(lab_row), jnp.zeros_like(lab)
    live = jnp.int32(0)
    for p in range(SLOTS):
        own = owner[p]
        slot_row = jnp.where(lab_row == p, own, slot_row)
        slot_col = jnp.where(lab == p, own, slot_col)
        live = live + jnp.where(own == slot, length[p], 0)
    place = (iota((PL, S), 0) == slot_row * CAP + rank_row).astype(BF16)
    unplace = (iota((S, PL), 1) == slot_col * CAP + rank_col).astype(BF16)

    for load in loads:
        load.wait()
    scale = (NOPE + ROPE) ** -0.5
    nope_s = dot(place, nope[...]).astype(BF16)
    rope_s = dot(place, rope[...]) * scale
    new_s = dot(place, new[...])
    new_s = jnp.concatenate([new_s[:, :LAT], jnp.concatenate([new_s[:, LAT:], jnp.zeros((PL, ROPE), F32)], axis=1)], axis=1)
    low = iota((PL, 2 * ROPE), 1) < ROPE
    for h in range(HL):
        rows = pl.ds(h, PL, stride=HL)
        lat_q = dot(nope_s[:, NOPE * h : NOPE * (h + 1)], ku[h]) * scale
        for j in range(4):
            stage[j, rows, :] = lat_q[:, 128 * j : 128 * j + 128]
        b = 128 * (h // 2)
        mine = rope_s[:, b : b + 128]
        if h % 2:
            mine = pltpu.roll(mine, ROPE, 1)
        if h < 9:
            piece = new_s[:, b : b + 128]
            if h % 2 == 0:
                piece = pltpu.roll(piece, ROPE, 1)
        else:
            piece = jnp.zeros_like(mine)
        stage[4, rows, :] = jnp.where(low, mine, piece)
    for j in range(5):
        qsend[:, pl.ds(128 * j, 128)] = stage[j].astype(BF16)

    def q_copy(s, d):
        return pltpu.make_async_remote_copy(
            src_ref=qsend.at[block(s)], dst_ref=q.at[block(r)], send_sem=qss.at[s], recv_sem=qrs.at[r], device_id=d, device_id_type=MESH
        )

    def q_dev(s):
        return dev(s // 4, ((s // 2) % 2) * 2 + s % 2, z, xl)

    own_q = pltpu.make_async_copy(qsend.at[block(r)], q.at[block(r)], qrs.at[r])

    def kv_copy(src, dst, sem, d):
        return pltpu.make_async_remote_copy(
            src_ref=kv.at[src], dst_ref=kv.at[dst], send_sem=kss.at[sem], recv_sem=krs.at[dst], device_id=d, device_id_type=MESH
        )

    o = jnp.where(role_a, 0, 16)

    def ring_own(u):
        return [kv_copy(o + u, o + 4 + u, u, zp), kv_copy(o + u, o + 8 + u, 4 + u, zm), kv_copy(o + u, o + u, 12 + u, sib)]

    def pair(j):
        if j < 2:
            return 2 * j, 2 * j + 1
        return (2 + j, 8 + (j - 2 ^ 1)) if j < 6 else (2 * j, 2 * j + 1)

    def ring_pass(j):
        a, b = pair(j)
        out_ = [kv_copy(o + k, o + k, 12 + k, sib) for k in (a, b)]
        if j in (2, 4):
            out_ = [kv_copy(o + a, o + 10 + j, 6 + j, zp), kv_copy(o + b, o + 11 + j, 7 + j, zm)] + out_
        return out_

    def arrived(k):
        kv_copy(k, k, 0, sib).wait_recv()

    def ring_step(j):
        for k in pair(j):
            arrived(o + k)
        for cp in ring_pass(j):
            cp.start()

    def cross_step(u):
        arrived(16 + u)
        for cp in ring_own(u):
            cp.start()

    cross = [kv_copy(32 + u, 16 + u, 28 + u, partner) for u in range(4)]

    pl.semaphore_wait(barrier, jnp.where(role_a, 25, 26))

    @pl.when(role_a)
    def _():
        by_part = [ring_own(u) for u in range(4)]
        for u in range(4):
            by_part[u][0].start()
            by_part[u ^ 1][1].start()
            by_part[u][2].start()

    def q_send(i, _):
        s = (slot + i) % SLOTS

        @pl.when(jnp.logical_and(role_a, i == 0))
        def _():
            own_q.start()

        @pl.when(jnp.logical_not(jnp.logical_and(role_a, i == 0)))
        def _():
            q_copy(s, q_dev(s)).start()
        return 0

    lax.fori_loop(0, SLOTS, q_send, 0)

    @pl.when(jnp.logical_not(role_a))
    def _():
        for cp in cross:
            cp.start()

    @pl.when(role_a)
    def _():
        for j in (2, 3, 4):
            ring_step(j)

    def q_wait(i, _):
        g = (r + i) % SLOTS

        @pl.when(jnp.logical_and(role_a, i == 0))
        def _():
            own_q.wait()

        @pl.when(jnp.logical_not(jnp.logical_and(role_a, i == 0)))
        def _():
            pltpu.make_async_remote_copy(
                src_ref=qsend.at[block(0)], dst_ref=q.at[block(g)], send_sem=qss.at[0], recv_sem=qrs.at[g], device_id=sib, device_id_type=MESH
            ).wait_recv()
        return 0

    lax.fori_loop(0, SLOTS, q_wait, 0)

    halves = [
        pltpu.make_async_remote_copy(
            src_ref=vu_h.at[pl.ds(8 * k, 8)], dst_ref=vu.at[pl.ds(8 * k, 8)], send_sem=vss.at[k], recv_sem=vrs.at[k],
            device_id=dev(y, (xh if k == 0 else 1 - xh) * 2 + 1 - xl, z, c), device_id_type=MESH,
        )
        for k in range(2)
    ]

    q3 = q[...]
    tail = q3[:, LAT:].astype(F32)
    wide_low = iota((ROWS, 2 * ROPE), 1) < ROPE
    stage[0] = tail
    tail = jnp.where(wide_low, tail, 0.0)
    pieces = [stage[0, pl.ds(k, PL, stride=HL), :] for k in range(9)]
    new_p = []
    for k in range(5):
        left = pltpu.roll(pieces[2 * k], ROPE, 1)
        new_p.append(jnp.where(low, left, pieces[2 * k + 1] if k < 4 else 0.0))
    new_p = jnp.concatenate(new_p, axis=1).astype(BF16)
    by_row = (iota((ROWS, PL), 0) // HL == iota((ROWS, PL), 1)).astype(BF16)
    own_keys = dot(by_row, new_p)
    own_score = jnp.sum(q3[:, :LAT].astype(F32) * own_keys[:, :LAT], axis=1, keepdims=True)
    own_score = own_score + jnp.sum(tail * own_keys[:, LAT:], axis=1, keepdims=True)
    for j in range(4):
        acc[j] = own_keys[:, 128 * j : 128 * j + 128]
    mtop[...] = jnp.broadcast_to(own_score, mtop.shape)
    tot[...] = (iota((ROWS, 128), 1) == 0).astype(F32)

    def attend(ka, kb):
        def first(k):
            s = k % 16 // 4
            zz = (z + jnp.where(s == 1, 3, jnp.where(s == 2, 1, jnp.where(s == 3, 2, 0)))) % 4
            return (zz * 2 + jnp.where(k < 16, xl, 1 - xl)) * SHARD + k % 4 * SUB

        keys = jnp.concatenate([kv[ka], kv[kb]], axis=1)
        lane = iota((1, CH), 1)
        at = lane + jnp.where(lane < SUB, first(ka), first(kb) - SUB)
        bias = jnp.where(at < live, 0.0, NEG)

        def score(b):
            return dot(q[pl.ds(b * RB, RB), pl.ds(0, KW)], keys) + bias

        following = score(0)
        for b in range(ROWS // RB):
            rs, s = pl.ds(b * RB, RB), following
            if (b + 1) * RB < ROWS:
                following = score(b + 1)
            tiles = [s[:, 128 * j : 128 * j + 128] for j in range(CH // 128)]
            top = mtop[rs, :]
            new_top = jnp.maximum(top, jnp.max(functools.reduce(jnp.maximum, tiles), axis=1, keepdims=True))
            shrink = jnp.exp(top - new_top)
            weights = [jnp.exp(a - new_top) for a in tiles]
            tot[rs, :] = tot[rs, :] * shrink + functools.reduce(jnp.add, weights)
            mtop[rs, :] = new_top
            new = dot_nt(jnp.concatenate([a.astype(BF16) for a in weights], axis=1), keys[:LAT])
            for j in range(4):
                acc[j, rs, :] = acc[j, rs, :] * shrink + new[:, 128 * j : 128 * j + 128]

    def step(i, _):
        j = i % 8
        inner = jnp.logical_and(j >= 2, j < 6)
        ka = jnp.where(inner, 2 + j, 2 * j) + i // 8 * 16
        kb = jnp.where(inner, 7 + j - j % 2 * 2, 2 * j + 1) + i // 8 * 16

        @pl.when(role_a)
        def _():
            for at, k in ((1, 5), (3, 6), (5, 7)):
                pl.when(i == at)(functools.partial(ring_step, k))

            @pl.when(i == 6)
            def _():
                for cp in halves:
                    cp.start()

            @pl.when(i >= 8)
            def _():
                arrived(ka)
                arrived(kb)

        @pl.when(jnp.logical_not(role_a))
        def _():
            @pl.when(i < 8)
            def _():
                arrived(ka)
                arrived(kb)

            for u in range(4):
                pl.when(i == 2 + 2 * u)(functools.partial(cross_step, u))
            for at, k in ((9, 2), (10, 3), (12, 4), (13, 5), (14, 6), (15, 7)):
                pl.when(i == at)(functools.partial(ring_step, k))

        attend(ka, kb)
        return 0

    lax.fori_loop(0, 16, step, 0)

    @pl.when(role_a)
    def _():
        vload.wait()

    @pl.when(jnp.logical_not(role_a))
    def _():
        for cp in halves:
            cp.wait_recv()

    for h in range(HL):
        rows = pl.ds(h, PL, stride=HL)
        total = jnp.sum(tot[rows, :], axis=1, keepdims=True)
        mean = jnp.concatenate([acc[j, rows, :] / total for j in range(4)], axis=1).astype(BF16)
        stage[0, rows, :] = dot(mean, vu[h])
    osend[...] = stage[0].astype(BF16)

    def o_copy(g):
        return pltpu.make_async_remote_copy(
            src_ref=osend.at[block(g)], dst_ref=orecv.at[block(slot)], send_sem=oss.at[g], recv_sem=ors.at[slot],
            device_id=(g, z * 2 + c), device_id_type=MESH,
        )

    own_o = pltpu.make_async_copy(osend.at[block(r)], orecv.at[block(r)], ors.at[r])

    def o_send(i, _):
        g = (r + i) % SLOTS
        kept = jnp.logical_and(role_a, i == 0)
        pl.when(kept)(own_o.start)
        pl.when(jnp.logical_not(kept))(lambda: o_copy(g).start())
        return 0

    lax.fori_loop(0, SLOTS, o_send, 0)

    @pl.when(role_a)
    def _():
        for cp in halves:
            cp.wait_send()

    @pl.when(jnp.logical_not(role_a))
    def _():
        for cp in cross:
            cp.wait_send()

    for u in range(4):
        for cp in ring_own(u):
            cp.wait_send()
    for j in range(2, 8):
        for cp in ring_pass(j):
            cp.wait_send()

    def all_wait(i, _):
        s = (slot + i) % SLOTS
        g = (r + i) % SLOTS
        kept = jnp.logical_and(role_a, i == 0)

        @pl.when(kept)
        def _():
            own_o.wait()

        @pl.when(jnp.logical_not(kept))
        def _():
            q_copy(s, sib).wait_send()
            o_copy(g).wait_send()
            pltpu.make_async_remote_copy(
                src_ref=osend.at[block(0)], dst_ref=orecv.at[block(s)], send_sem=oss.at[0], recv_sem=ors.at[s],
                device_id=sib, device_id_type=MESH,
            ).wait_recv()
        return 0

    lax.fori_loop(0, SLOTS, all_wait, 0)
    stage[0] = orecv[...].astype(F32)
    for h in range(HL):
        picked = stage[0, pl.ds(h, PL, stride=HL), :].astype(BF16)
        out[:, pl.ds(DV * h, DV)] = dot(unplace, picked).astype(BF16)


def shards(latent_cache, query_nope, query_rope, new_latent, key_up, value_up, prompt_owner, prompt_length, sample_prompt):
    hbm, smem, vmem = (pl.BlockSpec(memory_space=m) for m in (pl.ANY, pltpu.SMEM, pltpu.VMEM))
    dma = pltpu.SemaphoreType.DMA
    return pl.pallas_call(
        kernel,
        out_shape=jax.ShapeDtypeStruct(query_nope.shape, BF16),
        in_specs=[hbm] * 6 + [smem] * 2 + [vmem],
        out_specs=vmem,
        scratch_shapes=[
            pltpu.VMEM(query_nope.shape, BF16),
            pltpu.VMEM(query_rope.shape, BF16),
            pltpu.VMEM(new_latent.shape, BF16),
            pltpu.VMEM(key_up.shape, BF16),
            pltpu.VMEM(value_up.shape, BF16),
            pltpu.VMEM((36, KW, SUB), BF16),
            pltpu.VMEM((5, ROWS, 128), F32),
            pltpu.VMEM((ROWS, QW), BF16),
            pltpu.VMEM((ROWS, QW), BF16),
            pltpu.VMEM((ROWS, 128), F32),
            pltpu.VMEM((ROWS, 128), F32),
            pltpu.VMEM((4, ROWS, 128), F32),
            pltpu.VMEM((ROWS, DV), BF16),
            pltpu.VMEM((ROWS, DV), BF16),
            dma((9,)), dma((SLOTS,)), dma((SLOTS,)), dma((32,)), dma((32,)),
            dma((2,)), dma((2,)), dma((SLOTS,)), dma((SLOTS,)),
        ],
        compiler_params=pltpu.CompilerParams(collective_id=0, has_side_effects=True, vmem_limit_bytes=56 << 20),
        cost_estimate=pl.CostEstimate(flops=16 << 30, bytes_accessed=8 << 20, transcendentals=8 << 20),
    )(
        jnp.swapaxes(latent_cache, 1, 2), query_nope, query_rope, new_latent, key_up, value_up,
        prompt_owner, prompt_length, sample_prompt.reshape(1, -1),
    )


def solution(mesh):
    return jax.shard_map(
        shards,
        mesh=mesh,
        in_specs=(
            P("rep", "tp", None),
            P("rep", "tp"),
            P("rep", "tp"),
            P("rep", None),
            P("tp", None, None),
            P("tp", None, None),
            P(),
            P(),
            P("rep", None),
        ),
        out_specs=P("rep", "tp"),
        check_vma=False,
    )
```

```python
import functools

import jax
import jax.numpy as jnp
from jax import lax
from jax.experimental import pallas as pl
from jax.experimental.pallas import tpu as pltpu
from jax.sharding import PartitionSpec as P

MESH = pl.DeviceIdType.MESH
NEG = -1e30
F32, BF16 = jnp.float32, jnp.bfloat16

S, HL, SLOTS, CAP = 24, 16, 16, 3
PL = SLOTS * CAP
ROWS = PL * HL
LAT, ROPE, NOPE, DV = 512, 64, 128, 128
QW = LAT + 2 * ROPE
SHARD, SUB = 1024, 256
CH = 2 * SUB
KW = LAT + ROPE
RB = SLOTS * HL
NEAR_HEADS = 6
EARLY = 5


def dot(a, b):
    return jnp.dot(a, b, preferred_element_type=F32)


def dot_nt(a, b):
    return lax.dot_general(a, b, (((1,), (1,)), ((), ())), preferred_element_type=F32)


def swap(n, i):
    return sum((n // b % 2 + i // b % 2 - 2 * (n // b % 2) * (i // b % 2)) * b for b in (1, 2, 4, 8))


def block(i):
    return pl.ds(pl.multiple_of(i * HL, HL), HL)


def iota(shape, dim):
    return lax.broadcasted_iota(jnp.int32, shape, dim)


def kernel(
    latent, nope_h, rope_h, new_h, ku_h, vu_h, owner, length, labels, out,
    nope, rope, new, ku, vu, kv, stage, qsend, q, mtop, tot, acc, osend, orecv, unplace,
    lsem, qss, qrs, kss, krs, vss, vrs, oss, ors,
):
    r, t = lax.axis_index("rep"), lax.axis_index("tp")
    y, xh, c, z, xl = r // 4, (r // 2) % 2, r % 2, t // 2, t % 2
    role_a = c == xl

    def dev(yy, xx, zz, cc):
        return ((yy * 2 + xx // 2) * 2 + cc, zz * 2 + xx % 2)

    x = xh * 2 + xl
    zp, zm = dev(y, x, (z + 1) % 4, c), dev(y, x, (z + 3) % 4, c)
    sib = dev(y, x, z, 1 - c)
    partner = dev(y, xh * 2 + 1 - xl, z, 1 - c)
    slot = (y * 2 + xh) * 2 + xl

    base = jnp.where(role_a, 0, 32)
    loads = [
        pltpu.make_async_copy(nope_h, nope, lsem.at[0]),
        pltpu.make_async_copy(rope_h, rope, lsem.at[1]),
        pltpu.make_async_copy(new_h, new, lsem.at[2]),
        pltpu.make_async_copy(ku_h, ku, lsem.at[3]),
    ] + [pltpu.make_async_copy(latent.at[0, :, pl.ds(u * SUB, SUB)], kv.at[base + u], lsem.at[4 + u]) for u in range(4)]
    for load in loads:
        load.start()
    vload = pltpu.make_async_copy(vu_h, vu, lsem.at[8])
    pl.when(role_a)(vload.start)

    barrier = pltpu.get_barrier_semaphore()

    def greet_core(i, _):
        @pl.when(jnp.logical_not(jnp.logical_and(role_a, i == y * 4 + x)))
        def _():
            pl.semaphore_signal(barrier, inc=1, device_id=dev(i // 4, i % 4, z, xl), device_id_type=MESH)
        return 0

    def greet_col(i, _):
        pl.semaphore_signal(barrier, inc=1, device_id=dev(i // 2, (i % 2) * 2 + c, z, 1 - xl), device_id_type=MESH)
        return 0

    for d in (zp, zm):
        pl.semaphore_signal(barrier, inc=1, device_id=d, device_id_type=MESH)
    lax.fori_loop(0, 16, greet_core, 0)
    lax.fori_loop(0, 8, greet_col, 0)

    lab_row = labels[...]
    sub, lane = iota((S, S), 0), iota((S, S), 1)
    lab = jnp.sum(jnp.where(sub == lane, lab_row.astype(F32), 0.0), axis=1, keepdims=True).astype(jnp.int32)
    same = lab == lab_row
    rank_row = jnp.sum(jnp.where(same & (sub < lane), 1.0, 0.0), axis=0, keepdims=True).astype(jnp.int32)
    rank_col = jnp.sum(jnp.where(same & (lane < sub), 1.0, 0.0), axis=1, keepdims=True).astype(jnp.int32)
    slot_row, slot_col = jnp.zeros_like(lab_row), jnp.zeros_like(lab)
    live = jnp.int32(0)
    for p in range(SLOTS):
        own = owner[p]
        slot_row = jnp.where(lab_row == p, own, slot_row)
        slot_col = jnp.where(lab == p, own, slot_col)
        live = live + jnp.where(own == slot, length[p], 0)
    place = (iota((PL, S), 0) == rank_row * SLOTS + slot_row).astype(BF16)
    code = rank_col * SLOTS + slot_col

    for load in loads:
        load.wait()
    scale = (NOPE + ROPE) ** -0.5
    nope_s = dot(place, nope[...]).astype(BF16)
    rope_s = dot(place, rope[...]) * scale
    new_s = dot(place, new[...])
    new_s = jnp.concatenate([new_s[:, :LAT], jnp.concatenate([new_s[:, LAT:], jnp.zeros((PL, ROPE), F32)], axis=1)], axis=1)
    low = iota((PL, 2 * ROPE), 1) < ROPE
    def absorb(h):
        rows = pl.ds(h, PL, stride=HL)
        lat_q = dot(nope_s[:, NOPE * h : NOPE * (h + 1)], ku[h]) * scale
        for j in range(4):
            stage[j, rows, :] = lat_q[:, 128 * j : 128 * j + 128]
        b = 128 * (h // 2)
        mine = rope_s[:, b : b + 128]
        if h % 2:
            mine = pltpu.roll(mine, ROPE, 1)
        if h < 9:
            piece = new_s[:, b : b + 128]
            if h % 2 == 0:
                piece = pltpu.roll(piece, ROPE, 1)
        else:
            piece = jnp.zeros_like(mine)
        stage[4, rows, :] = jnp.where(low, mine, piece)
    for h in range(HL // 2):
        absorb(h)

    places = (pl.ds(0, 1), pl.ds(1, 2))

    def q_copy(n, s, d):
        return pltpu.make_async_remote_copy(
            src_ref=qsend.at[places[n], block(s)], dst_ref=q.at[places[n], block(r)],
            send_sem=qss.at[n * SLOTS + s], recv_sem=qrs.at[n * SLOTS + r], device_id=d, device_id_type=MESH,
        )

    def q_dev(s):
        return dev(s // 4, ((s // 2) % 2) * 2 + s % 2, z, xl)

    def own_q(n):
        return pltpu.make_async_copy(qsend.at[places[n], block(r)], q.at[places[n], block(r)], qrs.at[n * SLOTS + r])

    def kv_copy(src, dst, sem, d):
        return pltpu.make_async_remote_copy(
            src_ref=kv.at[src], dst_ref=kv.at[dst], send_sem=kss.at[sem], recv_sem=krs.at[dst], device_id=d, device_id_type=MESH
        )

    o = jnp.where(role_a, 0, 16)

    def ring_own(u):
        return [kv_copy(o + u, o + 4 + u, u, zp), kv_copy(o + u, o + 8 + u, 4 + u, zm), kv_copy(o + u, o + u, 12 + u, sib)]

    def pair(j):
        if j < 2:
            return 2 * j, 2 * j + 1
        return (2 + j, 8 + (j - 2 ^ 1)) if j < 6 else (2 * j, 2 * j + 1)

    def ring_pass(j):
        a, b = pair(j)
        out_ = [kv_copy(o + k, o + k, 12 + k, sib) for k in (a, b)]
        if j in (2, 4):
            out_ = [kv_copy(o + a, o + 10 + j, 6 + j, zp), kv_copy(o + b, o + 11 + j, 7 + j, zm)] + out_
        return out_

    def arrived(k):
        kv_copy(k, k, 0, sib).wait_recv()

    def ring_step(j):
        for k in pair(j):
            arrived(o + k)
        for cp in ring_pass(j):
            cp.start()

    def cross_step(u):
        arrived(16 + u)
        for cp in ring_own(u):
            cp.start()

    cross = [kv_copy(32 + u, 16 + u, 28 + u, partner) for u in range(4)]

    pl.semaphore_wait(barrier, jnp.where(role_a, 25, 26))

    @pl.when(role_a)
    def _():
        by_part = [ring_own(u) for u in range(4)]
        for u in range(4):
            by_part[u][0].start()
            by_part[u ^ 1][1].start()
            by_part[u][2].start()

    for h in range(HL // 2, HL):
        absorb(h)
    for j in range(5):
        qsend[:, :, pl.ds(128 * j, 128)] = stage[j].astype(BF16).reshape(CAP, RB, 128)

    def q_send(n, i, _):
        s = swap(slot, i)
        kept = jnp.logical_and(role_a, i == 0)
        pl.when(kept)(lambda: own_q(n).start())
        pl.when(jnp.logical_not(kept))(lambda: q_copy(n, s, q_dev(s)).start())
        return 0

    for n in range(2):
        lax.fori_loop(0, SLOTS, functools.partial(q_send, n), 0)

    @pl.when(jnp.logical_not(role_a))
    def _():
        for cp in cross:
            cp.start()

    def q_wait(n, i, _):
        g = (r + i) % SLOTS
        kept = jnp.logical_and(role_a, i == 0)
        pl.when(kept)(lambda: own_q(n).wait())

        @pl.when(jnp.logical_not(kept))
        def _():
            pltpu.make_async_remote_copy(
                src_ref=qsend.at[places[n], block(0)], dst_ref=q.at[places[n], block(g)],
                send_sem=qss.at[0], recv_sem=qrs.at[n * SLOTS + g], device_id=sib, device_id_type=MESH,
            ).wait_recv()
        return 0

    def value_part(k, first, count):
        return pltpu.make_async_remote_copy(
            src_ref=vu_h.at[pl.ds(first, count)], dst_ref=vu.at[pl.ds(first, count)], send_sem=vss.at[k], recv_sem=vrs.at[k],
            device_id=dev(y, (xh if k == 0 else 1 - xh) * 2 + 1 - xl, z, c), device_id_type=MESH,
        )

    halves = [value_part(0, 0, NEAR_HEADS), value_part(1, NEAR_HEADS, HL - NEAR_HEADS)]

    wanted = jnp.concatenate([code * HL + h for h in range(HL)], axis=0)
    unplace[...] = (iota((HL * S, ROWS), 1) == wanted).astype(BF16)

    low_b = low[:SLOTS]
    wide_low = iota((RB, 2 * ROPE), 1) < ROPE
    by_row = (iota((RB, SLOTS), 0) // HL == iota((RB, SLOTS), 1)).astype(BF16)

    def open_block(b):
        rs = pl.ds(b * RB, RB)
        qb = q[b]
        tail = qb[:, LAT:].astype(F32)
        stage[0, rs, :] = tail
        pieces = [stage[0, pl.ds(b * RB + k, SLOTS, stride=HL), :] for k in range(9)]
        new_p = []
        for k in range(5):
            left = pltpu.roll(pieces[2 * k], ROPE, 1)
            new_p.append(jnp.where(low_b, left, pieces[2 * k + 1] if k < 4 else 0.0))
        own_keys = dot(by_row, jnp.concatenate(new_p, axis=1).astype(BF16))
        own_score = jnp.sum(qb[:, :LAT].astype(F32) * own_keys[:, :LAT], axis=1, keepdims=True)
        own_score = own_score + jnp.sum(jnp.where(wide_low, tail, 0.0) * own_keys[:, LAT:], axis=1, keepdims=True)
        for j in range(4):
            acc[j, rs, :] = own_keys[:, 128 * j : 128 * j + 128]
        mtop[rs, :] = jnp.broadcast_to(own_score, (RB, 128))
        tot[rs, :] = (iota((RB, 128), 1) == 0).astype(F32)

    def attend(ka, kb, blocks):
        def first(k):
            s = k % 16 // 4
            zz = (z + jnp.where(s == 1, 3, jnp.where(s == 2, 1, jnp.where(s == 3, 2, 0)))) % 4
            return (zz * 2 + jnp.where(k < 16, xl, 1 - xl)) * SHARD + k % 4 * SUB

        keys = jnp.concatenate([kv[ka], kv[kb]], axis=1)
        lane = iota((1, CH), 1)
        at = lane + jnp.where(lane < SUB, first(ka), first(kb) - SUB)
        bias = jnp.where(at < live, 0.0, NEG)

        def score(b):
            return dot(q[b, :, pl.ds(0, KW)], keys) + bias

        following = score(blocks[0])
        for b in blocks:
            rs, s = pl.ds(b * RB, RB), following
            if b != blocks[-1]:
                following = score(b + 1)
            tiles = [s[:, 128 * j : 128 * j + 128] for j in range(CH // 128)]
            top = mtop[rs, :]
            new_top = jnp.maximum(top, jnp.max(functools.reduce(jnp.maximum, tiles), axis=1, keepdims=True))
            shrink = jnp.exp(top - new_top)
            weights = [jnp.exp(a - new_top) for a in tiles]
            tot[rs, :] = tot[rs, :] * shrink + functools.reduce(jnp.add, weights)
            mtop[rs, :] = new_top
            new = dot_nt(jnp.concatenate([a.astype(BF16) for a in weights], axis=1), keys[:LAT])
            for j in range(4):
                acc[j, rs, :] = acc[j, rs, :] * shrink + new[:, 128 * j : 128 * j + 128]

    turns_a = {0: {2: 2, 3: 3, 4: 4}, 1: {1: 5, 4: 6}, 2: {7: 7}}
    turns_x = {0: {}, 1: {2: 0, 4: 1}, 2: {7: 2, 8: 3}}
    turns_b = {0: {}, 1: {}, 2: {9: 2, 10: 3, 12: 4, 13: 5, 14: 6, 15: 7}}

    def step(loop, blocks, i, _):
        j = i % 8
        inner = jnp.logical_and(j >= 2, j < 6)
        ka = jnp.where(inner, 2 + j, 2 * j) + i // 8 * 16
        kb = jnp.where(inner, 7 + j - j % 2 * 2, 2 * j + 1) + i // 8 * 16

        def both():
            arrived(ka)
            arrived(kb)

        @pl.when(role_a)
        def _():
            for at, k in turns_a[loop].items():
                pl.when(i == at)(functools.partial(ring_step, k))
            if loop == 2:

                pl.when(i == 5)(halves[1].start)
                pl.when(i == 8)(halves[0].start)
                pl.when(i >= 8)(both)

        @pl.when(jnp.logical_not(role_a))
        def _():
            for at, k in turns_x[loop].items():
                pl.when(i == at)(functools.partial(cross_step, k))
            for at, k in turns_b[loop].items():
                pl.when(i == at)(functools.partial(ring_step, k))
            if loop == 0:
                both()
            if loop == 2:
                pl.when(i < 8)(both)

        attend(ka, kb, blocks)
        return 0

    lax.fori_loop(0, SLOTS, functools.partial(q_wait, 0), 0)
    open_block(0)
    lax.fori_loop(0, EARLY, functools.partial(step, 0, (0,)), 0)
    lax.fori_loop(0, SLOTS, functools.partial(q_wait, 1), 0)
    open_block(1)
    open_block(2)
    lax.fori_loop(0, EARLY, functools.partial(step, 1, (1, 2)), 0)
    lax.fori_loop(EARLY, 16, functools.partial(step, 2, (0, 1, 2)), 0)

    @pl.when(role_a)
    def _():
        vload.wait()

    @pl.when(jnp.logical_not(role_a))
    def _():
        for cp in halves:
            cp.wait_recv()

    for h in range(HL):
        rows = pl.ds(h, PL, stride=HL)
        share = 1.0 / jnp.sum(tot[rows, :], axis=1, keepdims=True)
        mean = jnp.concatenate([acc[j, rows, :] * share for j in range(4)], axis=1).astype(BF16)
        stage[0, rows, :] = dot(mean, vu[h])
    osend[...] = stage[0].astype(BF16).reshape(CAP, RB, DV)

    def o_copy(g):
        return pltpu.make_async_remote_copy(
            src_ref=osend.at[:, block(g)], dst_ref=orecv.at[:, block(slot)], send_sem=oss.at[g], recv_sem=ors.at[slot],
            device_id=(g, z * 2 + c), device_id_type=MESH,
        )

    own_o = pltpu.make_async_copy(osend.at[:, block(r)], orecv.at[:, block(r)], ors.at[r])

    def o_send(i, _):
        g = (r + i) % SLOTS
        kept = jnp.logical_and(role_a, i == 0)
        pl.when(kept)(own_o.start)
        pl.when(jnp.logical_not(kept))(lambda: o_copy(g).start())
        return 0

    lax.fori_loop(0, SLOTS, o_send, 0)

    @pl.when(role_a)
    def _():
        for cp in halves:
            cp.wait_send()

    @pl.when(jnp.logical_not(role_a))
    def _():
        for cp in cross:
            cp.wait_send()

    for u in range(4):
        for cp in ring_own(u):
            cp.wait_send()
    for j in range(2, 8):
        for cp in ring_pass(j):
            cp.wait_send()

    def all_wait(i, _):
        s = (slot + i) % SLOTS
        g = (r + i) % SLOTS
        kept = jnp.logical_and(role_a, i == 0)

        @pl.when(kept)
        def _():
            own_o.wait()

        @pl.when(jnp.logical_not(kept))
        def _():
            q_copy(0, s, sib).wait_send()
            q_copy(1, s, sib).wait_send()
            o_copy(g).wait_send()
            pltpu.make_async_remote_copy(
                src_ref=osend.at[:, block(0)], dst_ref=orecv.at[:, block(s)], send_sem=oss.at[0], recv_sem=ors.at[s],
                device_id=sib, device_id_type=MESH,
            ).wait_recv()
        return 0

    lax.fori_loop(0, SLOTS, all_wait, 0)
    picked = dot(unplace[...], orecv[...].reshape(ROWS, DV))
    for h in range(HL):
        out[:, pl.ds(DV * h, DV)] = picked[S * h : S * (h + 1)].astype(BF16)


def shards(latent_cache, query_nope, query_rope, new_latent, key_up, value_up, prompt_owner, prompt_length, sample_prompt):
    hbm, smem, vmem = (pl.BlockSpec(memory_space=m) for m in (pl.ANY, pltpu.SMEM, pltpu.VMEM))
    dma = pltpu.SemaphoreType.DMA
    return pl.pallas_call(
        kernel,
        out_shape=pltpu.VMEM(query_nope.shape, BF16),
        in_specs=[hbm] * 6 + [smem] * 2 + [vmem],
        out_specs=vmem,
        scratch_shapes=[
            pltpu.VMEM(query_nope.shape, BF16),
            pltpu.VMEM(query_rope.shape, BF16),
            pltpu.VMEM(new_latent.shape, BF16),
            pltpu.VMEM(key_up.shape, BF16),
            pltpu.VMEM(value_up.shape, BF16),
            pltpu.VMEM((36, KW, SUB), BF16),
            pltpu.VMEM((5, ROWS, 128), F32),
            pltpu.VMEM((CAP, RB, QW), BF16),
            pltpu.VMEM((CAP, RB, QW), BF16),
            pltpu.VMEM((ROWS, 128), F32),
            pltpu.VMEM((ROWS, 128), F32),
            pltpu.VMEM((4, ROWS, 128), F32),
            pltpu.VMEM((CAP, RB, DV), BF16),
            pltpu.VMEM((CAP, RB, DV), BF16),
            pltpu.VMEM((HL * S, ROWS), BF16),
            dma((9,)), dma((2 * SLOTS,)), dma((2 * SLOTS,)), dma((32,)), dma((32,)),
            dma((2,)), dma((2,)), dma((SLOTS,)), dma((SLOTS,)),
        ],
        compiler_params=pltpu.CompilerParams(collective_id=0, has_side_effects=True, vmem_limit_bytes=56 << 20),
        cost_estimate=pl.CostEstimate(flops=16 << 30, bytes_accessed=8 << 20, transcendentals=8 << 20),
    )(
        jnp.swapaxes(latent_cache, 1, 2), query_nope, query_rope, new_latent, key_up, value_up,
        prompt_owner, prompt_length, sample_prompt.reshape(1, -1),
    )


def solution(mesh):
    return jax.shard_map(
        shards,
        mesh=mesh,
        in_specs=(
            P("rep", "tp", None),
            P("rep", "tp"),
            P("rep", "tp"),
            P("rep", None),
            P("tp", None, None),
            P("tp", None, None),
            P(),
            P(),
            P("rep", None),
        ),
        out_specs=P("rep", "tp"),
        check_vma=False,
    )
```

```python
import functools

import jax
import jax.numpy as jnp
from jax import lax
from jax.experimental import pallas as pl
from jax.experimental.pallas import tpu as pltpu
from jax.sharding import PartitionSpec as P

MESH = pl.DeviceIdType.MESH
NEG = -1e30
F32, BF16 = jnp.float32, jnp.bfloat16

S, HL, SLOTS, CAP = 24, 16, 16, 3
PL = SLOTS * CAP
ROWS = PL * HL
LAT, ROPE, NOPE, DV = 512, 64, 128, 128
QW = LAT + 2 * ROPE
SHARD, SUB = 1024, 256
KW = LAT + ROPE
RB = SLOTS * HL
NEAR_HEADS = 6
EARLY = 5


def dot(a, b):
    return jnp.dot(a, b, preferred_element_type=F32)


def dot_nt(a, b):
    return lax.dot_general(a, b, (((1,), (1,)), ((), ())), preferred_element_type=F32)


def swap(n, i):
    return sum((n // b % 2 + i // b % 2 - 2 * (n // b % 2) * (i // b % 2)) * b for b in (1, 2, 4, 8))


def block(i):
    return pl.ds(pl.multiple_of(i * HL, HL), HL)


def iota(shape, dim):
    return lax.broadcasted_iota(jnp.int32, shape, dim)


def kernel(
    latent, nope_h, rope_h, new_h, ku_h, vu_h, owner_h, length_h, labels_h, out,
    labels, owner, length, nope, rope, new, ku, vu, kv, stage, qsend, q, mtop, tot, acc, osend, orecv, unplace,
    lsem, qss, qrs, kss, krs, vss, vrs, oss, ors,
):
    r, t = lax.axis_index("rep"), lax.axis_index("tp")
    y, xh, c, z, xl = r // 4, (r // 2) % 2, r % 2, t // 2, t % 2
    role_a = c == xl

    def dev(yy, xx, zz, cc):
        return ((yy * 2 + xx // 2) * 2 + cc, zz * 2 + xx % 2)

    x = xh * 2 + xl
    zp, zm = dev(y, x, (z + 1) % 4, c), dev(y, x, (z + 3) % 4, c)
    sib = dev(y, x, z, 1 - c)
    partner = dev(y, xh * 2 + 1 - xl, z, 1 - c)
    slot = (y * 2 + xh) * 2 + xl

    barrier = pltpu.get_barrier_semaphore()

    def greet(d):
        pl.semaphore_signal(barrier, inc=1, device_id=d, device_id_type=MESH)

    hops = (0, 1, 2, 1)
    for i in sorted(range(16), key=lambda i: -hops[i // 4] - hops[i % 4]):
        yy, xx = (y + i // 4) % 4, (x + i % 4) % 4
        if i == 0:
            pl.when(jnp.logical_not(role_a))(functools.partial(greet, dev(y, x, z, xl)))
        else:
            greet(dev(yy, xx, z, xl))
        if i % 2 == 0:
            greet(dev(yy, (xx + xl + c) % 4, z, 1 - xl))
    for d in (zp, zm):
        greet(d)

    base = jnp.where(role_a, 0, 32)
    loads = [
        pltpu.make_async_copy(nope_h, nope, lsem.at[0]),
        pltpu.make_async_copy(rope_h, rope, lsem.at[1]),
        pltpu.make_async_copy(new_h, new, lsem.at[2]),
        pltpu.make_async_copy(ku_h, ku, lsem.at[3]),
        pltpu.make_async_copy(labels_h, labels, lsem.at[9]),
        pltpu.make_async_copy(owner_h, owner, lsem.at[10]),
        pltpu.make_async_copy(length_h, length, lsem.at[11]),
    ] + [pltpu.make_async_copy(latent.at[0, :, pl.ds(u * SUB, SUB)], kv.at[base + u], lsem.at[4 + u]) for u in range(4)]
    for load in loads:
        load.start()
    vload = pltpu.make_async_copy(vu_h, vu, lsem.at[8])
    pl.when(role_a)(vload.start)

    for load in loads[4:7]:
        load.wait()
    lab_row = labels[...]
    sub, lane = iota((S, S), 0), iota((S, S), 1)
    lab = jnp.sum(jnp.where(sub == lane, lab_row.astype(F32), 0.0), axis=1, keepdims=True).astype(jnp.int32)
    same = lab == lab_row
    rank_row = jnp.sum(jnp.where(same & (sub < lane), 1.0, 0.0), axis=0, keepdims=True).astype(jnp.int32)
    rank_col = jnp.sum(jnp.where(same & (lane < sub), 1.0, 0.0), axis=1, keepdims=True).astype(jnp.int32)
    slot_row, slot_col = jnp.zeros_like(lab_row), jnp.zeros_like(lab)
    live = jnp.int32(0)
    for p in range(SLOTS):
        own = owner[p]
        slot_row = jnp.where(lab_row == p, own, slot_row)
        slot_col = jnp.where(lab == p, own, slot_col)
        live = live + jnp.where(own == slot, length[p], 0)
    place = (iota((PL, S), 0) == rank_row * SLOTS + slot_row).astype(BF16)
    code = rank_col * SLOTS + slot_col

    for load in loads[:4] + loads[7:]:
        load.wait()
    scale = (NOPE + ROPE) ** -0.5
    nope_s = dot(place, nope[...]).astype(BF16)
    rope_s = dot(place, rope[...]) * scale
    new_s = dot(place, new[...])
    new_s = jnp.concatenate([new_s[:, :LAT], jnp.concatenate([new_s[:, LAT:], jnp.zeros((PL, ROPE), F32)], axis=1)], axis=1)
    low = iota((PL, 2 * ROPE), 1) < ROPE
    def absorb(h):
        rows = pl.ds(h, PL, stride=HL)
        lat_q = dot(nope_s[:, NOPE * h : NOPE * (h + 1)], ku[h]) * scale
        for j in range(4):
            stage[j, rows, :] = lat_q[:, 128 * j : 128 * j + 128]
        b = 128 * (h // 2)
        mine = rope_s[:, b : b + 128]
        if h % 2:
            mine = pltpu.roll(mine, ROPE, 1)
        if h < 9:
            piece = new_s[:, b : b + 128]
            if h % 2 == 0:
                piece = pltpu.roll(piece, ROPE, 1)
        else:
            piece = jnp.zeros_like(mine)
        stage[4, rows, :] = jnp.where(low, mine, piece)
    for h in range(HL // 2):
        absorb(h)

    places = (pl.ds(0, 1), pl.ds(1, 2))

    def q_copy(n, s, d):
        return pltpu.make_async_remote_copy(
            src_ref=qsend.at[places[n], block(s)], dst_ref=q.at[places[n], block(r)],
            send_sem=qss.at[n * SLOTS + s], recv_sem=qrs.at[n * SLOTS + r], device_id=d, device_id_type=MESH,
        )

    def q_dev(s):
        return dev(s // 4, ((s // 2) % 2) * 2 + s % 2, z, xl)

    def own_q(n):
        return pltpu.make_async_copy(qsend.at[places[n], block(r)], q.at[places[n], block(r)], qrs.at[n * SLOTS + r])

    def kv_copy(src, dst, sem, d):
        return pltpu.make_async_remote_copy(
            src_ref=kv.at[src], dst_ref=kv.at[dst], send_sem=kss.at[sem], recv_sem=krs.at[dst], device_id=d, device_id_type=MESH
        )

    def half_copy(src, dst, half, sem, d):
        lanes = pl.ds(half * (SUB // 2), SUB // 2)
        return pltpu.make_async_remote_copy(
            src_ref=kv.at[src, :, lanes], dst_ref=kv.at[dst, :, lanes], send_sem=kss.at[sem],
            recv_sem=krs.at[dst if half == 0 else 32 + dst // 16 * 2 + dst % 2], device_id=d, device_id_type=MESH,
        )

    o = jnp.where(role_a, 0, 16)

    def ring_own(u):
        return [kv_copy(o + u, o + 4 + u, u, zp), kv_copy(o + u, o + 8 + u, 4 + u, zm), kv_copy(o + u, o + u, 12 + u, sib)]

    def pair(j):
        if j < 2:
            return 2 * j, 2 * j + 1
        return (2 + j, 8 + (j - 2 ^ 1)) if j < 6 else (2 * j, 2 * j + 1)

    def ring_pass(j):
        a, b = pair(j)
        out_ = [kv_copy(o + k, o + k, 12 + k, sib) for k in (a, b)]
        if j == 2:
            out_ = [kv_copy(o + a, o + 12, 8, zp), kv_copy(o + b, o + 13, 9, zm)] + out_
        if j == 4:
            halves_ = [(half_copy(o + a, o + 14, n, 10 + 22 * n, zp), half_copy(o + b, o + 15, n, 11 + 22 * n, zm)) for n in range(2)]
            out_ = [*halves_[0], *halves_[1]] + out_
        return out_

    def last_pass(n):
        return [half_copy(o + 14, o + 14, n, 26 + 8 * n, sib), half_copy(o + 15, o + 15, n, 27 + 8 * n, sib)]

    def arrived(k):
        kv_copy(k, k, 0, sib).wait_recv()

    def half_arrived(k, n):
        half_copy(k, k, n, 0, sib).wait_recv()

    def ring_step(j):
        for k in pair(j):
            arrived(o + k)
        for cp in ring_pass(j):
            cp.start()

    def last_step(n):
        half_arrived(o + 14, n)
        half_arrived(o + 15, n)
        for cp in last_pass(n):
            cp.start()

    def cross_step(u):
        arrived(16 + u)
        for cp in ring_own(u):
            cp.start()

    cross = [kv_copy(32 + u, 16 + u, 28 + u, partner) for u in range(4)]

    pl.semaphore_wait(barrier, jnp.where(role_a, 25, 26))

    @pl.when(role_a)
    def _():
        by_part = [ring_own(u) for u in range(4)]
        for u in range(4):
            by_part[u][0].start()
            by_part[u ^ 1][1].start()
            by_part[u][2].start()

    for h in range(HL // 2, HL):
        absorb(h)
    for j in range(5):
        qsend[:, :, pl.ds(128 * j, 128)] = stage[j].astype(BF16).reshape(CAP, RB, 128)

    def q_send(n, i, _):
        s = swap(slot, i)
        kept = jnp.logical_and(role_a, i == 0)
        pl.when(kept)(lambda: own_q(n).start())
        pl.when(jnp.logical_not(kept))(lambda: q_copy(n, s, q_dev(s)).start())
        return 0

    for n in range(2):
        lax.fori_loop(0, SLOTS, functools.partial(q_send, n), 0)

    @pl.when(jnp.logical_not(role_a))
    def _():
        for cp in cross:
            cp.start()

    def q_wait(n, i, _):
        g = (r + i) % SLOTS
        kept = jnp.logical_and(role_a, i == 0)
        pl.when(kept)(lambda: own_q(n).wait())

        @pl.when(jnp.logical_not(kept))
        def _():
            pltpu.make_async_remote_copy(
                src_ref=qsend.at[places[n], block(0)], dst_ref=q.at[places[n], block(g)],
                send_sem=qss.at[0], recv_sem=qrs.at[n * SLOTS + g], device_id=sib, device_id_type=MESH,
            ).wait_recv()
        return 0

    def value_part(k, first, count):
        return pltpu.make_async_remote_copy(
            src_ref=vu_h.at[pl.ds(first, count)], dst_ref=vu.at[pl.ds(first, count)], send_sem=vss.at[k], recv_sem=vrs.at[k],
            device_id=dev(y, (xh if k == 0 else 1 - xh) * 2 + 1 - xl, z, c), device_id_type=MESH,
        )

    halves = [value_part(0, 0, NEAR_HEADS), value_part(1, NEAR_HEADS, HL - NEAR_HEADS)]

    wanted = jnp.concatenate([code * HL + h for h in range(HL)], axis=0)
    unplace[...] = (iota((HL * S, ROWS), 1) == wanted).astype(BF16)

    low_b = low[:SLOTS]
    wide_low = iota((RB, 2 * ROPE), 1) < ROPE
    by_row = (iota((RB, SLOTS), 0) // HL == iota((RB, SLOTS), 1)).astype(BF16)

    def open_block(b):
        rs = pl.ds(b * RB, RB)
        qb = q[b]
        tail = qb[:, LAT:].astype(F32)
        stage[0, rs, :] = tail
        pieces = [stage[0, pl.ds(b * RB + k, SLOTS, stride=HL), :] for k in range(9)]
        new_p = []
        for k in range(5):
            left = pltpu.roll(pieces[2 * k], ROPE, 1)
            new_p.append(jnp.where(low_b, left, pieces[2 * k + 1] if k < 4 else 0.0))
        own_keys = dot(by_row, jnp.concatenate(new_p, axis=1).astype(BF16))
        own_score = jnp.sum(qb[:, :LAT].astype(F32) * own_keys[:, :LAT], axis=1, keepdims=True)
        own_score = own_score + jnp.sum(jnp.where(wide_low, tail, 0.0) * own_keys[:, LAT:], axis=1, keepdims=True)
        for j in range(4):
            acc[j, rs, :] = own_keys[:, 128 * j : 128 * j + 128]
        mtop[rs, :] = jnp.broadcast_to(own_score, (RB, 128))
        tot[rs, :] = (iota((RB, 128), 1) == 0).astype(F32)

    def first(k):
        s = k % 16 // 4
        zz = (z + jnp.where(s == 1, 3, jnp.where(s == 2, 1, jnp.where(s == 3, 2, 0)))) % 4
        return (zz * 2 + jnp.where(k < 16, xl, 1 - xl)) * SHARD + k % 4 * SUB

    def attend(ka, kb, blocks, start=0, width=SUB):
        lanes = pl.ds(start, width)
        keys = jnp.concatenate([kv[ka, :, lanes], kv[kb, :, lanes]], axis=1)
        lane = iota((1, 2 * width), 1)
        at = lane + start + jnp.where(lane < width, first(ka), first(kb) - width)
        bias = jnp.where(at < live, 0.0, NEG)

        def score(b):
            return dot(q[b, :, pl.ds(0, KW)], keys) + bias

        following = score(blocks[0])
        for b in blocks:
            rs, s = pl.ds(b * RB, RB), following
            if b != blocks[-1]:
                following = score(b + 1)
            tiles = [s[:, 128 * j : 128 * j + 128] for j in range(2 * width // 128)]
            top = mtop[rs, :]
            new_top = jnp.maximum(top, jnp.max(functools.reduce(jnp.maximum, tiles), axis=1, keepdims=True))
            shrink = jnp.exp(top - new_top)
            weights = [jnp.exp(a - new_top) for a in tiles]
            tot[rs, :] = tot[rs, :] * shrink + functools.reduce(jnp.add, weights)
            mtop[rs, :] = new_top
            new = dot_nt(jnp.concatenate([a.astype(BF16) for a in weights], axis=1), keys[:LAT])
            for j in range(4):
                acc[j, rs, :] = acc[j, rs, :] * shrink + new[:, 128 * j : 128 * j + 128]

    turns_a = {0: {2: 2, 3: 3, 4: 4}, 1: {1: 5, 4: 6}, 2: {}}
    turns_x = {0: {}, 1: {2: 0, 4: 1}, 2: {7: 2, 8: 3}}
    turns_b = {0: {}, 1: {}, 2: {9: 2, 10: 3, 12: 4, 13: 5, 14: 6}}

    def step(loop, blocks, i, _):
        j = i % 8
        inner = jnp.logical_and(j >= 2, j < 6)
        ka = jnp.where(inner, 2 + j, 2 * j) + i // 8 * 16
        kb = jnp.where(inner, 7 + j - j % 2 * 2, 2 * j + 1) + i // 8 * 16

        def both():
            arrived(ka)
            arrived(kb)

        @pl.when(role_a)
        def _():
            for at, k in turns_a[loop].items():
                pl.when(i == at)(functools.partial(ring_step, k))
            if loop == 2:

                @pl.when(i == 7)
                def _():
                    last_step(0)
                    last_step(1)

                pl.when(i == 5)(halves[1].start)
                pl.when(i == 8)(halves[0].start)
                pl.when(i >= 8)(both)

        @pl.when(jnp.logical_not(role_a))
        def _():
            for at, k in turns_x[loop].items():
                pl.when(i == at)(functools.partial(cross_step, k))
            for at, k in turns_b[loop].items():
                pl.when(i == at)(functools.partial(ring_step, k))
            if loop == 0:
                both()
            if loop == 2:
                pl.when(i < 7)(both)

                @pl.when(i == 7)
                def _():
                    for n in range(2):
                        half_arrived(14, n)
                        half_arrived(15, n)

        attend(ka, kb, blocks)
        return 0

    lax.fori_loop(0, SLOTS, functools.partial(q_wait, 0), 0)
    open_block(0)
    lax.fori_loop(0, EARLY, functools.partial(step, 0, (0,)), 0)
    lax.fori_loop(0, SLOTS, functools.partial(q_wait, 1), 0)
    open_block(1)
    open_block(2)
    lax.fori_loop(0, EARLY, functools.partial(step, 1, (1, 2)), 0)
    lax.fori_loop(EARLY, 15, functools.partial(step, 2, (0, 1, 2)), 0)
    for n in range(2):
        pl.when(jnp.logical_not(role_a))(functools.partial(last_step, n))

        @pl.when(role_a)
        def _():
            half_arrived(30, n)
            half_arrived(31, n)

        attend(30, 31, (0, 1, 2), n * (SUB // 2), SUB // 2)

    @pl.when(role_a)
    def _():
        vload.wait()

    @pl.when(jnp.logical_not(role_a))
    def _():
        for cp in halves:
            cp.wait_recv()

    for h in range(HL):
        rows = pl.ds(h, PL, stride=HL)
        share = 1.0 / jnp.sum(tot[rows, :], axis=1, keepdims=True)
        mean = jnp.concatenate([acc[j, rows, :] * share for j in range(4)], axis=1).astype(BF16)
        stage[0, rows, :] = dot(mean, vu[h])
    osend[...] = stage[0].astype(BF16).reshape(CAP, RB, DV)

    def o_copy(g):
        return pltpu.make_async_remote_copy(
            src_ref=osend.at[:, block(g)], dst_ref=orecv.at[:, block(slot)], send_sem=oss.at[g], recv_sem=ors.at[slot],
            device_id=(g, z * 2 + c), device_id_type=MESH,
        )

    own_o = pltpu.make_async_copy(osend.at[:, block(r)], orecv.at[:, block(r)], ors.at[r])

    def o_send(i, _):
        g = (r + i) % SLOTS
        kept = jnp.logical_and(role_a, i == 0)
        pl.when(kept)(own_o.start)
        pl.when(jnp.logical_not(kept))(lambda: o_copy(g).start())
        return 0

    lax.fori_loop(0, SLOTS, o_send, 0)

    @pl.when(role_a)
    def _():
        for cp in halves:
            cp.wait_send()

    @pl.when(jnp.logical_not(role_a))
    def _():
        for cp in cross:
            cp.wait_send()

    for u in range(4):
        for cp in ring_own(u):
            cp.wait_send()
    for j in range(2, 7):
        for cp in ring_pass(j):
            cp.wait_send()
    for n in range(2):
        for cp in last_pass(n):
            cp.wait_send()

    def all_wait(i, _):
        s = (slot + i) % SLOTS
        g = (r + i) % SLOTS
        kept = jnp.logical_and(role_a, i == 0)

        @pl.when(kept)
        def _():
            own_o.wait()

        @pl.when(jnp.logical_not(kept))
        def _():
            q_copy(0, s, sib).wait_send()
            q_copy(1, s, sib).wait_send()
            o_copy(g).wait_send()
            pltpu.make_async_remote_copy(
                src_ref=osend.at[:, block(0)], dst_ref=orecv.at[:, block(s)], send_sem=oss.at[0], recv_sem=ors.at[s],
                device_id=sib, device_id_type=MESH,
            ).wait_recv()
        return 0

    lax.fori_loop(0, SLOTS, all_wait, 0)
    picked = dot(unplace[...], orecv[...].reshape(ROWS, DV))
    for h in range(HL):
        out[:, pl.ds(DV * h, DV)] = picked[S * h : S * (h + 1)].astype(BF16)


def shards(latent_cache, query_nope, query_rope, new_latent, key_up, value_up, prompt_owner, prompt_length, sample_prompt):
    hbm, vmem = (pl.BlockSpec(memory_space=m) for m in (pl.ANY, pltpu.VMEM))
    dma = pltpu.SemaphoreType.DMA
    return pl.pallas_call(
        kernel,
        out_shape=pltpu.VMEM(query_nope.shape, BF16),
        in_specs=[hbm] * 9,
        out_specs=vmem,
        scratch_shapes=[
            pltpu.VMEM((1, S), jnp.int32),
            pltpu.SMEM((SLOTS,), jnp.int32),
            pltpu.SMEM((SLOTS,), jnp.int32),
            pltpu.VMEM(query_nope.shape, BF16),
            pltpu.VMEM(query_rope.shape, BF16),
            pltpu.VMEM(new_latent.shape, BF16),
            pltpu.VMEM(key_up.shape, BF16),
            pltpu.VMEM(value_up.shape, BF16),
            pltpu.VMEM((36, KW, SUB), BF16),
            pltpu.VMEM((5, ROWS, 128), F32),
            pltpu.VMEM((CAP, RB, QW), BF16),
            pltpu.VMEM((CAP, RB, QW), BF16),
            pltpu.VMEM((ROWS, 128), F32),
            pltpu.VMEM((ROWS, 128), F32),
            pltpu.VMEM((4, ROWS, 128), F32),
            pltpu.VMEM((CAP, RB, DV), BF16),
            pltpu.VMEM((CAP, RB, DV), BF16),
            pltpu.VMEM((HL * S, ROWS), BF16),
            dma((12,)), dma((2 * SLOTS,)), dma((2 * SLOTS,)), dma((36,)), dma((36,)),
            dma((2,)), dma((2,)), dma((SLOTS,)), dma((SLOTS,)),
        ],
        compiler_params=pltpu.CompilerParams(collective_id=0, has_side_effects=True, vmem_limit_bytes=56 << 20),
        cost_estimate=pl.CostEstimate(flops=16 << 30, bytes_accessed=8 << 20, transcendentals=8 << 20),
    )(
        jnp.swapaxes(latent_cache, 1, 2), query_nope, query_rope, new_latent, key_up, value_up,
        prompt_owner, prompt_length, sample_prompt.reshape(1, -1),
    )


def solution(mesh):
    return jax.shard_map(
        shards,
        mesh=mesh,
        in_specs=(
            P("rep", "tp", None),
            P("rep", "tp"),
            P("rep", "tp"),
            P("rep", None),
            P("tp", None, None),
            P("tp", None, None),
            P(),
            P(),
            P("rep", None),
        ),
        out_specs=P("rep", "tp"),
        check_vma=False,
    )
```

```python
import functools

import jax
import jax.numpy as jnp
from jax import lax
from jax.experimental import pallas as pl
from jax.experimental.pallas import tpu as pltpu
from jax.sharding import PartitionSpec as P

MESH = pl.DeviceIdType.MESH
NEG = -1e30
F32, BF16 = jnp.float32, jnp.bfloat16

S, HL, SLOTS, CAP = 24, 16, 16, 3
PL = SLOTS * CAP
ROWS = PL * HL
LAT, ROPE, NOPE, DV = 512, 64, 128, 128
QW = LAT + 2 * ROPE
SHARD, SUB = 1024, 256
KW = LAT + ROPE
RB = SLOTS * HL
NEAR_HEADS = 6
EARLY = 5


def dot(a, b):
    return jnp.dot(a, b, preferred_element_type=F32)


def dot_nt(a, b):
    return lax.dot_general(a, b, (((1,), (1,)), ((), ())), preferred_element_type=F32)


def swap(n, i):
    return sum((n // b % 2 + i // b % 2 - 2 * (n // b % 2) * (i // b % 2)) * b for b in (1, 2, 4, 8))


def block(i):
    return pl.ds(pl.multiple_of(i * HL, HL), HL)


def iota(shape, dim):
    return lax.broadcasted_iota(jnp.int32, shape, dim)


def kernel(
    latent, nope_h, rope_h, new_h, ku_h, vu_h, owner_h, length_h, labels_h, out,
    labels, owner, length, nope, rope, new, ku, vu, kv, stage, qsend, q, mtop, tot, acc, osend, orecv, unplace,
    lsem, qss, qrs, kss, krs, vss, vrs, oss, ors,
):
    r, t = lax.axis_index("rep"), lax.axis_index("tp")
    y, xh, c, z, xl = r // 4, (r // 2) % 2, r % 2, t // 2, t % 2
    role_a = c == xl

    def dev(yy, xx, zz, cc):
        return ((yy * 2 + xx // 2) * 2 + cc, zz * 2 + xx % 2)

    x = xh * 2 + xl
    zp, zm = dev(y, x, (z + 1) % 4, c), dev(y, x, (z + 3) % 4, c)
    sib = dev(y, x, z, 1 - c)
    partner = dev(y, xh * 2 + 1 - xl, z, 1 - c)
    slot = (y * 2 + xh) * 2 + xl

    barrier = pltpu.get_barrier_semaphore()

    def greet(d):
        pl.semaphore_signal(barrier, inc=1, device_id=d, device_id_type=MESH)

    hops = (0, 1, 2, 1)
    for i in sorted(range(16), key=lambda i: -hops[i // 4] - hops[i % 4]):
        yy, xx = (y + i // 4) % 4, (x + i % 4) % 4
        if i == 0:
            pl.when(jnp.logical_not(role_a))(functools.partial(greet, dev(y, x, z, xl)))
        else:
            greet(dev(yy, xx, z, xl))
        if i % 2 == 0:
            greet(dev(yy, (xx + xl + c) % 4, z, 1 - xl))
    for d in (zp, zm):
        greet(d)

    base = jnp.where(role_a, 0, 32)
    loads = [
        pltpu.make_async_copy(nope_h, nope, lsem.at[0]),
        pltpu.make_async_copy(rope_h, rope, lsem.at[1]),
        pltpu.make_async_copy(new_h, new, lsem.at[2]),
        pltpu.make_async_copy(ku_h, ku, lsem.at[3]),
        pltpu.make_async_copy(labels_h, labels, lsem.at[9]),
        pltpu.make_async_copy(owner_h, owner, lsem.at[10]),
        pltpu.make_async_copy(length_h, length, lsem.at[11]),
    ] + [pltpu.make_async_copy(latent.at[0, :, pl.ds(u * SUB, SUB)], kv.at[base + u], lsem.at[4 + u]) for u in range(4)]
    for load in loads:
        load.start()
    vload = pltpu.make_async_copy(vu_h, vu, lsem.at[8])
    pl.when(role_a)(vload.start)

    for load in loads[4:7]:
        load.wait()
    lab_row = labels[...]
    sub, lane = iota((S, S), 0), iota((S, S), 1)
    lab = jnp.sum(jnp.where(sub == lane, lab_row.astype(F32), 0.0), axis=1, keepdims=True).astype(jnp.int32)
    same = lab == lab_row
    rank_row = jnp.sum(jnp.where(same & (sub < lane), 1.0, 0.0), axis=0, keepdims=True).astype(jnp.int32)
    rank_col = jnp.sum(jnp.where(same & (lane < sub), 1.0, 0.0), axis=1, keepdims=True).astype(jnp.int32)
    slot_row, slot_col = jnp.zeros_like(lab_row), jnp.zeros_like(lab)
    live = jnp.int32(0)
    for p in range(SLOTS):
        own = owner[p]
        slot_row = jnp.where(lab_row == p, own, slot_row)
        slot_col = jnp.where(lab == p, own, slot_col)
        live = live + jnp.where(own == slot, length[p], 0)
    place = (iota((PL, S), 0) == rank_row * SLOTS + slot_row).astype(BF16)
    code = rank_col * SLOTS + slot_col

    for load in loads[:4] + loads[7:]:
        load.wait()
    scale = (NOPE + ROPE) ** -0.5
    nope_s = dot(place, nope[...]).astype(BF16)
    rope_s = dot(place, rope[...]) * scale
    new_s = dot(place, new[...])
    new_s = jnp.concatenate([new_s[:, :LAT], jnp.concatenate([new_s[:, LAT:], jnp.zeros((PL, ROPE), F32)], axis=1)], axis=1)
    low = iota((PL, 2 * ROPE), 1) < ROPE
    def absorb(h):
        rows = pl.ds(h, PL, stride=HL)
        lat_q = dot(nope_s[:, NOPE * h : NOPE * (h + 1)], ku[h]) * scale
        for j in range(4):
            stage[j, rows, :] = lat_q[:, 128 * j : 128 * j + 128]
        b = 128 * (h // 2)
        mine = rope_s[:, b : b + 128]
        if h % 2:
            mine = pltpu.roll(mine, ROPE, 1)
        if h < 9:
            piece = new_s[:, b : b + 128]
            if h % 2 == 0:
                piece = pltpu.roll(piece, ROPE, 1)
        else:
            piece = jnp.zeros_like(mine)
        stage[4, rows, :] = jnp.where(low, mine, piece)
    for h in range(HL // 4):
        absorb(h)

    places = (pl.ds(0, 1), pl.ds(1, 2))

    def q_copy(n, s, d):
        return pltpu.make_async_remote_copy(
            src_ref=qsend.at[places[n], block(s)], dst_ref=q.at[places[n], block(r)],
            send_sem=qss.at[n * SLOTS + s], recv_sem=qrs.at[n * SLOTS + r], device_id=d, device_id_type=MESH,
        )

    def q_dev(s):
        return dev(s // 4, ((s // 2) % 2) * 2 + s % 2, z, xl)

    def own_q(n):
        return pltpu.make_async_copy(qsend.at[places[n], block(r)], q.at[places[n], block(r)], qrs.at[n * SLOTS + r])

    def kv_copy(src, dst, sem, d):
        return pltpu.make_async_remote_copy(
            src_ref=kv.at[src], dst_ref=kv.at[dst], send_sem=kss.at[sem], recv_sem=krs.at[dst], device_id=d, device_id_type=MESH
        )

    def half_copy(src, dst, half, sem, d):
        lanes = pl.ds(half * (SUB // 2), SUB // 2)
        return pltpu.make_async_remote_copy(
            src_ref=kv.at[src, :, lanes], dst_ref=kv.at[dst, :, lanes], send_sem=kss.at[sem],
            recv_sem=krs.at[dst if half == 0 else 32 + dst // 16 * 2 + dst % 2], device_id=d, device_id_type=MESH,
        )

    o = jnp.where(role_a, 0, 16)

    def ring_own(u):
        return [kv_copy(o + u, o + 4 + u, u, zp), kv_copy(o + u, o + 8 + u, 4 + u, zm), kv_copy(o + u, o + u, 12 + u, sib)]

    def pair(j):
        if j < 2:
            return 2 * j, 2 * j + 1
        return (2 + j, 8 + (j - 2 ^ 1)) if j < 6 else (2 * j, 2 * j + 1)

    def ring_pass(j):
        a, b = pair(j)
        out_ = [kv_copy(o + k, o + k, 12 + k, sib) for k in (a, b)]
        if j == 2:
            out_ = [kv_copy(o + a, o + 12, 8, zp), kv_copy(o + b, o + 13, 9, zm)] + out_
        if j == 4:
            halves_ = [(half_copy(o + a, o + 14, n, 10 + 22 * n, zp), half_copy(o + b, o + 15, n, 11 + 22 * n, zm)) for n in range(2)]
            out_ = [*halves_[0], *halves_[1]] + out_
        return out_

    def last_pass(n):
        return [half_copy(o + 14, o + 14, n, 26 + 8 * n, sib), half_copy(o + 15, o + 15, n, 27 + 8 * n, sib)]

    def arrived(k):
        kv_copy(k, k, 0, sib).wait_recv()

    def half_arrived(k, n):
        half_copy(k, k, n, 0, sib).wait_recv()

    def ring_step(j):
        for k in pair(j):
            arrived(o + k)
        for cp in ring_pass(j):
            cp.start()

    def last_step(n):
        half_arrived(o + 14, n)
        half_arrived(o + 15, n)
        for cp in last_pass(n):
            cp.start()

    def cross_step(u):
        arrived(16 + u)
        for cp in ring_own(u):
            cp.start()

    cross = [kv_copy(32 + u, 16 + u, 28 + u, partner) for u in range(4)]

    pl.semaphore_wait(barrier, jnp.where(role_a, 25, 26))

    @pl.when(role_a)
    def _():
        by_part = [ring_own(u) for u in range(4)]
        for u in range(4):
            by_part[u][0].start()
            by_part[u ^ 1][1].start()
            by_part[u][2].start()

    for h in range(HL // 4, HL):
        absorb(h)
    for j in range(5):
        qsend[:, :, pl.ds(128 * j, 128)] = stage[j].astype(BF16).reshape(CAP, RB, 128)

    def q_send(n, i, _):
        s = swap(slot, i)
        kept = jnp.logical_and(role_a, i == 0)
        pl.when(kept)(lambda: own_q(n).start())
        pl.when(jnp.logical_not(kept))(lambda: q_copy(n, s, q_dev(s)).start())
        return 0

    for n in range(2):
        lax.fori_loop(0, SLOTS, functools.partial(q_send, n), 0)

    @pl.when(jnp.logical_not(role_a))
    def _():
        for cp in cross:
            cp.start()

    def q_wait(n, i, _):
        g = (r + i) % SLOTS
        kept = jnp.logical_and(role_a, i == 0)
        pl.when(kept)(lambda: own_q(n).wait())

        @pl.when(jnp.logical_not(kept))
        def _():
            pltpu.make_async_remote_copy(
                src_ref=qsend.at[places[n], block(0)], dst_ref=q.at[places[n], block(g)],
                send_sem=qss.at[0], recv_sem=qrs.at[n * SLOTS + g], device_id=sib, device_id_type=MESH,
            ).wait_recv()
        return 0

    def value_part(k, first, count):
        return pltpu.make_async_remote_copy(
            src_ref=vu_h.at[pl.ds(first, count)], dst_ref=vu.at[pl.ds(first, count)], send_sem=vss.at[k], recv_sem=vrs.at[k],
            device_id=dev(y, (xh if k == 0 else 1 - xh) * 2 + 1 - xl, z, c), device_id_type=MESH,
        )

    halves = [value_part(0, 0, NEAR_HEADS), value_part(1, NEAR_HEADS, HL - NEAR_HEADS)]

    wanted = jnp.concatenate([code * HL + h for h in range(HL)], axis=0)
    unplace[...] = (iota((HL * S, ROWS), 1) == wanted).astype(BF16)

    low_b = low[:SLOTS]
    wide_low = iota((RB, 2 * ROPE), 1) < ROPE
    by_row = (iota((RB, SLOTS), 0) // HL == iota((RB, SLOTS), 1)).astype(BF16)

    def open_block(b):
        rs = pl.ds(b * RB, RB)
        qb = q[b]
        tail = qb[:, LAT:].astype(F32)
        stage[0, rs, :] = tail
        pieces = [stage[0, pl.ds(b * RB + k, SLOTS, stride=HL), :] for k in range(9)]
        new_p = []
        for k in range(5):
            left = pltpu.roll(pieces[2 * k], ROPE, 1)
            new_p.append(jnp.where(low_b, left, pieces[2 * k + 1] if k < 4 else 0.0))
        own_keys = dot(by_row, jnp.concatenate(new_p, axis=1).astype(BF16))
        own_score = jnp.sum(qb[:, :LAT].astype(F32) * own_keys[:, :LAT], axis=1, keepdims=True)
        own_score = own_score + jnp.sum(jnp.where(wide_low, tail, 0.0) * own_keys[:, LAT:], axis=1, keepdims=True)
        for j in range(4):
            acc[j, rs, :] = own_keys[:, 128 * j : 128 * j + 128]
        mtop[rs, :] = jnp.broadcast_to(own_score, (RB, 128))
        tot[rs, :] = (iota((RB, 128), 1) == 0).astype(F32)

    def first(k):
        s = k % 16 // 4
        zz = (z + jnp.where(s == 1, 3, jnp.where(s == 2, 1, jnp.where(s == 3, 2, 0)))) % 4
        return (zz * 2 + jnp.where(k < 16, xl, 1 - xl)) * SHARD + k % 4 * SUB

    def attend(ka, kb, blocks, start=0, width=SUB):
        lanes = pl.ds(start, width)
        keys = jnp.concatenate([kv[ka, :, lanes], kv[kb, :, lanes]], axis=1)
        lane = iota((1, 2 * width), 1)
        at = lane + start + jnp.where(lane < width, first(ka), first(kb) - width)
        bias = jnp.where(at < live, 0.0, NEG)

        scores = [dot(q[b, :, pl.ds(0, KW)], keys) + bias for b in blocks]
        shrinks, weights_bf = [], []
        for b, s in zip(blocks, scores):
            rs = pl.ds(b * RB, RB)
            tiles = [s[:, 128 * j : 128 * j + 128] for j in range(2 * width // 128)]
            top = mtop[rs, :]
            new_top = jnp.maximum(top, jnp.max(functools.reduce(jnp.maximum, tiles), axis=1, keepdims=True))
            shrink = jnp.exp(top - new_top)
            weights = [jnp.exp(a - new_top) for a in tiles]
            tot[rs, :] = tot[rs, :] * shrink + functools.reduce(jnp.add, weights)
            mtop[rs, :] = new_top
            shrinks.append(shrink)
            weights_bf.append(jnp.concatenate([a.astype(BF16) for a in weights], axis=1))
        for b, shrink, w in zip(blocks, shrinks, weights_bf):
            rs = pl.ds(b * RB, RB)
            new = dot_nt(w, keys[:LAT])
            for j in range(4):
                acc[j, rs, :] = acc[j, rs, :] * shrink + new[:, 128 * j : 128 * j + 128]

    turns_a = {0: {2: 2, 3: 3, 4: 4}, 1: {1: 5, 4: 6}, 2: {}}
    turns_x = {0: {}, 1: {2: 0, 4: 1}, 2: {7: 2, 8: 3}}
    turns_b = {0: {}, 1: {}, 2: {9: 2, 10: 3, 12: 4, 13: 5, 14: 6}}

    def step(loop, blocks, i, _):
        j = i % 8
        inner = jnp.logical_and(j >= 2, j < 6)
        ka = jnp.where(inner, 2 + j, 2 * j) + i // 8 * 16
        kb = jnp.where(inner, 7 + j - j % 2 * 2, 2 * j + 1) + i // 8 * 16

        def both():
            arrived(ka)
            arrived(kb)

        @pl.when(role_a)
        def _():
            for at, k in turns_a[loop].items():
                pl.when(i == at)(functools.partial(ring_step, k))
            if loop == 2:

                @pl.when(i == 7)
                def _():
                    last_step(0)
                    last_step(1)

                pl.when(i == 5)(halves[1].start)
                pl.when(i == 8)(halves[0].start)
                pl.when(i >= 8)(both)

        @pl.when(jnp.logical_not(role_a))
        def _():
            for at, k in turns_x[loop].items():
                pl.when(i == at)(functools.partial(cross_step, k))
            for at, k in turns_b[loop].items():
                pl.when(i == at)(functools.partial(ring_step, k))
            if loop == 0:
                both()
            if loop == 2:
                pl.when(i < 7)(both)

                @pl.when(i == 7)
                def _():
                    for n in range(2):
                        half_arrived(14, n)
                        half_arrived(15, n)

        attend(ka, kb, blocks)
        return 0

    lax.fori_loop(0, SLOTS, functools.partial(q_wait, 0), 0)
    open_block(0)
    lax.fori_loop(0, EARLY, functools.partial(step, 0, (0,)), 0)
    lax.fori_loop(0, SLOTS, functools.partial(q_wait, 1), 0)
    open_block(1)
    open_block(2)
    lax.fori_loop(0, EARLY, functools.partial(step, 1, (1, 2)), 0)
    lax.fori_loop(EARLY, 15, functools.partial(step, 2, (0, 1, 2)), 0)
    for n in range(2):
        pl.when(jnp.logical_not(role_a))(functools.partial(last_step, n))

        @pl.when(role_a)
        def _():
            half_arrived(30, n)
            half_arrived(31, n)

        attend(30, 31, (0, 1, 2), n * (SUB // 2), SUB // 2)

    @pl.when(role_a)
    def _():
        vload.wait()

    @pl.when(jnp.logical_not(role_a))
    def _():
        for cp in halves:
            cp.wait_recv()

    for h in range(HL):
        rows = pl.ds(h, PL, stride=HL)
        share = 1.0 / jnp.sum(tot[rows, :], axis=1, keepdims=True)
        mean = jnp.concatenate([acc[j, rows, :] * share for j in range(4)], axis=1).astype(BF16)
        stage[0, rows, :] = dot(mean, vu[h])
    osend[...] = stage[0].astype(BF16).reshape(CAP, RB, DV)

    def o_copy(g):
        return pltpu.make_async_remote_copy(
            src_ref=osend.at[:, block(g)], dst_ref=orecv.at[:, block(slot)], send_sem=oss.at[g], recv_sem=ors.at[slot],
            device_id=(g, z * 2 + c), device_id_type=MESH,
        )

    own_o = pltpu.make_async_copy(osend.at[:, block(r)], orecv.at[:, block(r)], ors.at[r])

    for iy in (2, 1, 3, 0):
        for ix, ic in ((1, 0), (1, 1), (0, 0), (0, 1)):
            g = ((y + iy) % 4 * 2 + (xh + ix) % 2) * 2 + (c + ic) % 2
            if iy + ix + ic:
                o_copy(g).start()
            else:
                pl.when(role_a)(own_o.start)
                pl.when(jnp.logical_not(role_a))(o_copy(g).start)

    @pl.when(role_a)
    def _():
        for cp in halves:
            cp.wait_send()

    @pl.when(jnp.logical_not(role_a))
    def _():
        for cp in cross:
            cp.wait_send()

    for u in range(4):
        for cp in ring_own(u):
            cp.wait_send()
    for j in range(2, 7):
        for cp in ring_pass(j):
            cp.wait_send()
    for n in range(2):
        for cp in last_pass(n):
            cp.wait_send()

    def all_wait(i, _):
        s = (slot + i) % SLOTS
        g = (r + i) % SLOTS
        kept = jnp.logical_and(role_a, i == 0)

        @pl.when(kept)
        def _():
            own_o.wait()

        @pl.when(jnp.logical_not(kept))
        def _():
            q_copy(0, s, sib).wait_send()
            q_copy(1, s, sib).wait_send()
            o_copy(g).wait_send()
            pltpu.make_async_remote_copy(
                src_ref=osend.at[:, block(0)], dst_ref=orecv.at[:, block(s)], send_sem=oss.at[0], recv_sem=ors.at[s],
                device_id=sib, device_id_type=MESH,
            ).wait_recv()
        return 0

    lax.fori_loop(0, SLOTS, all_wait, 0)
    picked = dot(unplace[...], orecv[...].reshape(ROWS, DV))
    for h in range(HL):
        out[:, pl.ds(DV * h, DV)] = picked[S * h : S * (h + 1)].astype(BF16)


def shards(latent_cache, query_nope, query_rope, new_latent, key_up, value_up, prompt_owner, prompt_length, sample_prompt):
    hbm, vmem = (pl.BlockSpec(memory_space=m) for m in (pl.ANY, pltpu.VMEM))
    dma = pltpu.SemaphoreType.DMA
    return pl.pallas_call(
        kernel,
        out_shape=pltpu.VMEM(query_nope.shape, BF16),
        in_specs=[hbm] * 9,
        out_specs=vmem,
        scratch_shapes=[
            pltpu.VMEM((1, S), jnp.int32),
            pltpu.SMEM((SLOTS,), jnp.int32),
            pltpu.SMEM((SLOTS,), jnp.int32),
            pltpu.VMEM(query_nope.shape, BF16),
            pltpu.VMEM(query_rope.shape, BF16),
            pltpu.VMEM(new_latent.shape, BF16),
            pltpu.VMEM(key_up.shape, BF16),
            pltpu.VMEM(value_up.shape, BF16),
            pltpu.VMEM((36, KW, SUB), BF16),
            pltpu.VMEM((5, ROWS, 128), F32),
            pltpu.VMEM((CAP, RB, QW), BF16),
            pltpu.VMEM((CAP, RB, QW), BF16),
            pltpu.VMEM((ROWS, 128), F32),
            pltpu.VMEM((ROWS, 128), F32),
            pltpu.VMEM((4, ROWS, 128), F32),
            pltpu.VMEM((CAP, RB, DV), BF16),
            pltpu.VMEM((CAP, RB, DV), BF16),
            pltpu.VMEM((HL * S, ROWS), BF16),
            dma((12,)), dma((2 * SLOTS,)), dma((2 * SLOTS,)), dma((36,)), dma((36,)),
            dma((2,)), dma((2,)), dma((SLOTS,)), dma((SLOTS,)),
        ],
        compiler_params=pltpu.CompilerParams(collective_id=0, has_side_effects=True, vmem_limit_bytes=56 << 20),
        cost_estimate=pl.CostEstimate(flops=16 << 30, bytes_accessed=8 << 20, transcendentals=8 << 20),
    )(
        jnp.swapaxes(latent_cache, 1, 2), query_nope, query_rope, new_latent, key_up, value_up,
        prompt_owner, prompt_length, sample_prompt.reshape(1, -1),
    )


def solution(mesh):
    return jax.shard_map(
        shards,
        mesh=mesh,
        in_specs=(
            P("rep", "tp", None),
            P("rep", "tp"),
            P("rep", "tp"),
            P("rep", None),
            P("tp", None, None),
            P("tp", None, None),
            P(),
            P(),
            P("rep", None),
        ),
        out_specs=P("rep", "tp"),
        check_vma=False,
    )
```

```python
import functools

import jax
import jax.numpy as jnp
from jax import lax
from jax.experimental import pallas as pl
from jax.experimental.pallas import tpu as pltpu
from jax.sharding import PartitionSpec as P

MESH = pl.DeviceIdType.MESH
NEG = -1e30
F32, BF16 = jnp.float32, jnp.bfloat16

S, HL, SLOTS, CAP = 24, 16, 16, 3
PL = SLOTS * CAP
ROWS = PL * HL
LAT, ROPE, NOPE, DV = 512, 64, 128, 128
QW = LAT + 2 * ROPE
SHARD, SUB = 1024, 256
KW = LAT + ROPE
RB = SLOTS * HL
NEAR_HEADS = 6
EARLY = 5


def dot(a, b):
    return jnp.dot(a, b, preferred_element_type=F32)


def dot_nt(a, b):
    return lax.dot_general(a, b, (((1,), (1,)), ((), ())), preferred_element_type=F32)


def swap(n, i):
    return sum((n // b % 2 + i // b % 2 - 2 * (n // b % 2) * (i // b % 2)) * b for b in (1, 2, 4, 8))


def block(i):
    return pl.ds(pl.multiple_of(i * HL, HL), HL)


def iota(shape, dim):
    return lax.broadcasted_iota(jnp.int32, shape, dim)


def kernel(
    latent, nope_h, rope_h, new_h, ku_h, vu_h, owner_h, length_h, labels_h, out,
    labels, owner, length, nope, rope, new, ku, vu, kv, stage, qsend, q, mtop, tot, acc, osend, orecv, unplace,
    lsem, qss, qrs, kss, krs, vss, vrs, oss, ors,
):
    r, t = lax.axis_index("rep"), lax.axis_index("tp")
    y, xh, c, z, xl = r // 4, (r // 2) % 2, r % 2, t // 2, t % 2
    role_a = c == xl

    def dev(yy, xx, zz, cc):
        return ((yy * 2 + xx // 2) * 2 + cc, zz * 2 + xx % 2)

    x = xh * 2 + xl
    zp, zm = dev(y, x, (z + 1) % 4, c), dev(y, x, (z + 3) % 4, c)
    sib = dev(y, x, z, 1 - c)
    partner = dev(y, xh * 2 + 1 - xl, z, 1 - c)
    slot = (y * 2 + xh) * 2 + xl

    barrier = pltpu.get_barrier_semaphore()

    def greet(d):
        pl.semaphore_signal(barrier, inc=1, device_id=d, device_id_type=MESH)

    hops = (0, 1, 2, 1)
    for i in sorted(range(16), key=lambda i: -hops[i // 4] - hops[i % 4]):
        yy, xx = (y + i // 4) % 4, (x + i % 4) % 4
        if i == 0:
            pl.when(jnp.logical_not(role_a))(functools.partial(greet, dev(y, x, z, xl)))
        else:
            greet(dev(yy, xx, z, xl))
        if i % 2 == 0:
            greet(dev(yy, (xx + xl + c) % 4, z, 1 - xl))
    for d in (zp, zm):
        greet(d)

    base = jnp.where(role_a, 0, 32)
    loads = [
        pltpu.make_async_copy(nope_h, nope, lsem.at[0]),
        pltpu.make_async_copy(rope_h, rope, lsem.at[1]),
        pltpu.make_async_copy(new_h, new, lsem.at[2]),
        pltpu.make_async_copy(ku_h, ku, lsem.at[3]),
        pltpu.make_async_copy(labels_h, labels, lsem.at[9]),
        pltpu.make_async_copy(owner_h, owner, lsem.at[10]),
        pltpu.make_async_copy(length_h, length, lsem.at[11]),
    ] + [pltpu.make_async_copy(latent.at[0, :, pl.ds(u * SUB, SUB)], kv.at[base + u], lsem.at[4 + u]) for u in range(4)]
    for load in loads:
        load.start()
    vload = pltpu.make_async_copy(vu_h, vu, lsem.at[8])
    pl.when(role_a)(vload.start)

    for load in loads[4:7]:
        load.wait()
    lab_row = labels[...]
    sub, lane = iota((S, S), 0), iota((S, S), 1)
    lab = jnp.sum(jnp.where(sub == lane, lab_row.astype(F32), 0.0), axis=1, keepdims=True).astype(jnp.int32)
    same = lab == lab_row
    rank_row = jnp.sum(jnp.where(same & (sub < lane), 1.0, 0.0), axis=0, keepdims=True).astype(jnp.int32)
    rank_col = jnp.sum(jnp.where(same & (lane < sub), 1.0, 0.0), axis=1, keepdims=True).astype(jnp.int32)
    slot_row, slot_col = jnp.zeros_like(lab_row), jnp.zeros_like(lab)
    live = jnp.int32(0)
    for p in range(SLOTS):
        own = owner[p]
        slot_row = jnp.where(lab_row == p, own, slot_row)
        slot_col = jnp.where(lab == p, own, slot_col)
        live = live + jnp.where(own == slot, length[p], 0)
    place = (iota((PL, S), 0) == rank_row * SLOTS + slot_row).astype(BF16)
    code = rank_col * SLOTS + slot_col

    for load in loads[:4] + loads[7:]:
        load.wait()
    scale = (NOPE + ROPE) ** -0.5
    nope_s = dot(place, nope[...]).astype(BF16)
    rope_s = dot(place, rope[...]) * scale
    new_s = dot(place, new[...])
    new_s = jnp.concatenate([new_s[:, :LAT], jnp.concatenate([new_s[:, LAT:], jnp.zeros((PL, ROPE), F32)], axis=1)], axis=1)
    low = iota((PL, 2 * ROPE), 1) < ROPE
    def absorb(h):
        rows = pl.ds(h, PL, stride=HL)
        lat_q = dot(nope_s[:, NOPE * h : NOPE * (h + 1)], ku[h]) * scale
        for j in range(4):
            stage[j, rows, :] = lat_q[:, 128 * j : 128 * j + 128]
        b = 128 * (h // 2)
        mine = rope_s[:, b : b + 128]
        if h % 2:
            mine = pltpu.roll(mine, ROPE, 1)
        if h < 9:
            piece = new_s[:, b : b + 128]
            if h % 2 == 0:
                piece = pltpu.roll(piece, ROPE, 1)
        else:
            piece = jnp.zeros_like(mine)
        stage[4, rows, :] = jnp.where(low, mine, piece)
    for h in range(HL // 4):
        absorb(h)

    places = (pl.ds(0, 1), pl.ds(1, 2))

    def q_copy(n, s, d):
        return pltpu.make_async_remote_copy(
            src_ref=qsend.at[places[n], block(s)], dst_ref=q.at[places[n], block(r)],
            send_sem=qss.at[n * SLOTS + s], recv_sem=qrs.at[n * SLOTS + r], device_id=d, device_id_type=MESH,
        )

    def q_dev(s):
        return dev(s // 4, ((s // 2) % 2) * 2 + s % 2, z, xl)

    def own_q(n):
        return pltpu.make_async_copy(qsend.at[places[n], block(r)], q.at[places[n], block(r)], qrs.at[n * SLOTS + r])

    def kv_copy(src, dst, sem, d):
        return pltpu.make_async_remote_copy(
            src_ref=kv.at[src], dst_ref=kv.at[dst], send_sem=kss.at[sem], recv_sem=krs.at[dst], device_id=d, device_id_type=MESH
        )

    def half_copy(src, dst, half, sem, d):
        lanes = pl.ds(half * (SUB // 2), SUB // 2)
        return pltpu.make_async_remote_copy(
            src_ref=kv.at[src, :, lanes], dst_ref=kv.at[dst, :, lanes], send_sem=kss.at[sem],
            recv_sem=krs.at[dst if half == 0 else 32 + dst // 16 * 2 + dst % 2], device_id=d, device_id_type=MESH,
        )

    o = jnp.where(role_a, 0, 16)

    def ring_own(u):
        return [kv_copy(o + u, o + 4 + u, u, zp), kv_copy(o + u, o + 8 + u, 4 + u, zm), kv_copy(o + u, o + u, 12 + u, sib)]

    def pair(j):
        if j < 2:
            return 2 * j, 2 * j + 1
        return (2 + j, 8 + (j - 2 ^ 1)) if j < 6 else (2 * j, 2 * j + 1)

    def ring_pass(j):
        a, b = pair(j)
        on_a, on_b = ([kv_copy(o + k, o + k, 12 + k, sib)] for k in (a, b))
        if j == 2:
            on_a = [kv_copy(o + a, o + 12, 8, zp)] + on_a
            on_b = [kv_copy(o + b, o + 13, 9, zm)] + on_b
        if j == 4:
            on_a = [half_copy(o + a, o + 14, n, 10 + 22 * n, zp) for n in range(2)] + on_a
            on_b = [half_copy(o + b, o + 15, n, 11 + 22 * n, zm) for n in range(2)] + on_b
        return on_a, on_b

    def last_pass(n):
        return [half_copy(o + 14, o + 14, n, 26 + 8 * n, sib), half_copy(o + 15, o + 15, n, 27 + 8 * n, sib)]

    def arrived(k):
        kv_copy(k, k, 0, sib).wait_recv()

    def half_arrived(k, n):
        half_copy(k, k, n, 0, sib).wait_recv()

    def ring_step(j):
        for k, onward in zip(pair(j), ring_pass(j)):
            arrived(o + k)
            for cp in onward:
                cp.start()

    def last_step(n):
        for k, cp in zip((14, 15), last_pass(n)):
            half_arrived(o + k, n)
            cp.start()

    def cross_step(u):
        arrived(16 + u)
        for cp in ring_own(u):
            cp.start()

    cross = [kv_copy(32 + u, 16 + u, 28 + u, partner) for u in range(4)]

    pl.semaphore_wait(barrier, jnp.where(role_a, 25, 26))

    @pl.when(role_a)
    def _():
        by_part = [ring_own(u) for u in range(4)]
        for u in range(4):
            by_part[u][0].start()
            by_part[u ^ 1][1].start()
            by_part[u][2].start()

    for h in range(HL // 4, HL):
        absorb(h)
    for j in range(5):
        qsend[:, :, pl.ds(128 * j, 128)] = stage[j, pl.ds(0, ROWS), :].astype(BF16).reshape(CAP, RB, 128)

    def q_send(n, i, _):
        s = swap(slot, i)
        kept = jnp.logical_and(role_a, i == 0)
        pl.when(kept)(lambda: own_q(n).start())
        pl.when(jnp.logical_not(kept))(lambda: q_copy(n, s, q_dev(s)).start())
        return 0

    for n in range(2):
        lax.fori_loop(0, SLOTS, functools.partial(q_send, n), 0)

    @pl.when(jnp.logical_not(role_a))
    def _():
        for cp in cross:
            cp.start()

    def q_wait(n, i, _):
        g = (r + i) % SLOTS
        kept = jnp.logical_and(role_a, i == 0)
        pl.when(kept)(lambda: own_q(n).wait())

        @pl.when(jnp.logical_not(kept))
        def _():
            pltpu.make_async_remote_copy(
                src_ref=qsend.at[places[n], block(0)], dst_ref=q.at[places[n], block(g)],
                send_sem=qss.at[0], recv_sem=qrs.at[n * SLOTS + g], device_id=sib, device_id_type=MESH,
            ).wait_recv()
        return 0

    def value_part(k, first, count):
        return pltpu.make_async_remote_copy(
            src_ref=vu_h.at[pl.ds(first, count)], dst_ref=vu.at[pl.ds(first, count)], send_sem=vss.at[k], recv_sem=vrs.at[k],
            device_id=dev(y, (xh if k == 0 else 1 - xh) * 2 + 1 - xl, z, c), device_id_type=MESH,
        )

    halves = [value_part(0, 0, NEAR_HEADS), value_part(1, NEAR_HEADS, HL - NEAR_HEADS)]

    wanted = jnp.concatenate([code * HL + h for h in range(HL)], axis=0)
    unplace[...] = (iota((HL * S, ROWS), 1) == wanted).astype(BF16)

    low_b = low[:SLOTS]
    wide_low = iota((RB, 2 * ROPE), 1) < ROPE
    by_row = (iota((RB, SLOTS), 0) // HL == iota((RB, SLOTS), 1)).astype(BF16)

    def open_block(b):
        rs = pl.ds(b * RB, RB)
        qb = q[b]
        tail = qb[:, LAT:].astype(F32)
        stage[0, rs, :] = tail
        pieces = [stage[0, pl.ds(b * RB + k, SLOTS, stride=HL), :] for k in range(9)]
        new_p = []
        for k in range(5):
            left = pltpu.roll(pieces[2 * k], ROPE, 1)
            new_p.append(jnp.where(low_b, left, pieces[2 * k + 1] if k < 4 else 0.0))
        own_keys = dot(by_row, jnp.concatenate(new_p, axis=1).astype(BF16))
        own_score = jnp.sum(qb[:, :LAT].astype(F32) * own_keys[:, :LAT], axis=1, keepdims=True)
        own_score = own_score + jnp.sum(jnp.where(wide_low, tail, 0.0) * own_keys[:, LAT:], axis=1, keepdims=True)
        for j in range(4):
            acc[j, rs, :] = own_keys[:, 128 * j : 128 * j + 128]
        mtop[rs, :] = jnp.broadcast_to(own_score, (RB, 128))
        tot[rs, :] = (iota((RB, 128), 1) == 0).astype(F32)

    def first(k):
        s = k % 16 // 4
        zz = (z + jnp.where(s == 1, 3, jnp.where(s == 2, 1, jnp.where(s == 3, 2, 0)))) % 4
        return (zz * 2 + jnp.where(k < 16, xl, 1 - xl)) * SHARD + k % 4 * SUB

    def attend(ka, kb, blocks, start=0, width=SUB):
        lanes = pl.ds(start, width)
        keys = jnp.concatenate([kv[ka, :, lanes], kv[kb, :, lanes]], axis=1)
        lane = iota((1, 2 * width), 1)
        at = lane + start + jnp.where(lane < width, first(ka), first(kb) - width)
        bias = jnp.where(at < live, 0.0, NEG)

        scores = [dot(q[b, :, pl.ds(0, KW)], keys) + bias for b in blocks]
        shrinks, weights_bf = [], []
        for b, s in zip(blocks, scores):
            rs = pl.ds(b * RB, RB)
            tiles = [s[:, 128 * j : 128 * j + 128] for j in range(2 * width // 128)]
            top = mtop[rs, :]
            new_top = jnp.maximum(top, jnp.max(functools.reduce(jnp.maximum, tiles), axis=1, keepdims=True))
            shrink = jnp.exp(top - new_top)
            weights = [jnp.exp(a - new_top) for a in tiles]
            tot[rs, :] = tot[rs, :] * shrink + functools.reduce(jnp.add, weights)
            mtop[rs, :] = new_top
            shrinks.append(shrink)
            weights_bf.append(jnp.concatenate([a.astype(BF16) for a in weights], axis=1))
        for b, shrink, w in zip(blocks, shrinks, weights_bf):
            rs = pl.ds(b * RB, RB)
            new = dot_nt(w, keys[:LAT])
            for j in range(4):
                acc[j, rs, :] = acc[j, rs, :] * shrink + new[:, 128 * j : 128 * j + 128]

    turns_a = {0: {2: 2, 3: 3, 4: 4}, 1: {1: 5, 4: 6}, 2: {}}
    turns_x = {0: {}, 1: {2: 0, 4: 1}, 2: {7: 2, 8: 3}}
    turns_b = {0: {}, 1: {}, 2: {9: 2, 10: 3, 12: 4, 13: 5, 14: 6}}

    def step(loop, blocks, i, _):
        j = i % 8
        inner = jnp.logical_and(j >= 2, j < 6)
        ka = jnp.where(inner, 2 + j, 2 * j) + i // 8 * 16
        kb = jnp.where(inner, 7 + j - j % 2 * 2, 2 * j + 1) + i // 8 * 16

        def both():
            arrived(ka)
            arrived(kb)

        @pl.when(role_a)
        def _():
            for at, k in turns_a[loop].items():
                pl.when(i == at)(functools.partial(ring_step, k))
            if loop == 2:

                @pl.when(i == 7)
                def _():
                    last_step(0)
                    last_step(1)

                pl.when(i == 5)(halves[1].start)
                pl.when(i == 8)(halves[0].start)
                pl.when(i >= 8)(both)

        @pl.when(jnp.logical_not(role_a))
        def _():
            for at, k in turns_x[loop].items():
                pl.when(i == at)(functools.partial(cross_step, k))
            for at, k in turns_b[loop].items():
                pl.when(i == at)(functools.partial(ring_step, k))
            if loop == 0:
                both()
            if loop == 2:
                pl.when(i < 7)(both)

                @pl.when(i == 7)
                def _():
                    for n in range(2):
                        half_arrived(14, n)
                        half_arrived(15, n)

        attend(ka, kb, blocks)
        return 0

    lax.fori_loop(0, SLOTS, functools.partial(q_wait, 0), 0)
    open_block(0)
    lax.fori_loop(0, EARLY, functools.partial(step, 0, (0,)), 0)
    lax.fori_loop(0, SLOTS, functools.partial(q_wait, 1), 0)
    open_block(1)
    open_block(2)
    lax.fori_loop(0, EARLY, functools.partial(step, 1, (1, 2)), 0)
    lax.fori_loop(EARLY, 15, functools.partial(step, 2, (0, 1, 2)), 0)
    for n in range(2):
        pl.when(jnp.logical_not(role_a))(functools.partial(last_step, n))

        @pl.when(role_a)
        def _():
            half_arrived(30, n)
            half_arrived(31, n)

        attend(30, 31, (0, 1, 2), n * (SUB // 2), SUB // 2)

    @pl.when(role_a)
    def _():
        vload.wait()

    @pl.when(jnp.logical_not(role_a))
    def _():
        for cp in halves:
            cp.wait_recv()

    for h in range(HL):
        rows = pl.ds(h, PL, stride=HL)
        share = 1.0 / jnp.sum(tot[rows, :], axis=1, keepdims=True)
        mean = jnp.concatenate([acc[j, rows, :] * share for j in range(4)], axis=1).astype(BF16)
        stage[0, rows, :] = dot(mean, vu[h])
    osend[...] = stage[0, pl.ds(0, ROWS), :].astype(BF16).reshape(CAP, RB, DV)

    def o_copy(g):
        return pltpu.make_async_remote_copy(
            src_ref=osend.at[:, block(g)], dst_ref=orecv.at[:, block(slot)], send_sem=oss.at[g], recv_sem=ors.at[slot],
            device_id=(g, z * 2 + c), device_id_type=MESH,
        )

    own_o = pltpu.make_async_copy(osend.at[:, block(r)], orecv.at[:, block(r)], ors.at[r])

    for iy in (2, 1, 3, 0):
        for ix, ic in ((1, 0), (1, 1), (0, 0), (0, 1)):
            g = ((y + iy) % 4 * 2 + (xh + ix) % 2) * 2 + (c + ic) % 2
            if iy + ix + ic:
                o_copy(g).start()
            else:
                pl.when(role_a)(own_o.start)
                pl.when(jnp.logical_not(role_a))(o_copy(g).start)

    @pl.when(role_a)
    def _():
        for cp in halves:
            cp.wait_send()

    @pl.when(jnp.logical_not(role_a))
    def _():
        for cp in cross:
            cp.wait_send()

    for u in range(4):
        for cp in ring_own(u):
            cp.wait_send()
    for j in range(2, 7):
        for onward in ring_pass(j):
            for cp in onward:
                cp.wait_send()
    for n in range(2):
        for cp in last_pass(n):
            cp.wait_send()

    def all_wait(i, _):
        s = (slot + i) % SLOTS
        g = (r + i) % SLOTS
        kept = jnp.logical_and(role_a, i == 0)

        @pl.when(kept)
        def _():
            own_o.wait()

        @pl.when(jnp.logical_not(kept))
        def _():
            q_copy(0, s, sib).wait_send()
            q_copy(1, s, sib).wait_send()
            o_copy(g).wait_send()
            pltpu.make_async_remote_copy(
                src_ref=osend.at[:, block(0)], dst_ref=orecv.at[:, block(s)], send_sem=oss.at[0], recv_sem=ors.at[s],
                device_id=sib, device_id_type=MESH,
            ).wait_recv()
        return 0

    lax.fori_loop(0, SLOTS, all_wait, 0)
    picked = dot(unplace[...], orecv[...].reshape(ROWS, DV))
    for h in range(HL):
        out[:, pl.ds(DV * h, DV)] = picked[S * h : S * (h + 1)].astype(BF16)


def shards(latent_cache, query_nope, query_rope, new_latent, key_up, value_up, prompt_owner, prompt_length, sample_prompt):
    hbm, vmem = (pl.BlockSpec(memory_space=m) for m in (pl.ANY, pltpu.VMEM))
    dma = pltpu.SemaphoreType.DMA
    return pl.pallas_call(
        kernel,
        out_shape=pltpu.VMEM(query_nope.shape, BF16),
        in_specs=[hbm] * 9,
        out_specs=vmem,
        scratch_shapes=[
            pltpu.VMEM((1, S), jnp.int32),
            pltpu.SMEM((SLOTS,), jnp.int32),
            pltpu.SMEM((SLOTS,), jnp.int32),
            pltpu.VMEM(query_nope.shape, BF16),
            pltpu.VMEM(query_rope.shape, BF16),
            pltpu.VMEM(new_latent.shape, BF16),
            pltpu.VMEM(key_up.shape, BF16),
            pltpu.VMEM(value_up.shape, BF16),
            pltpu.VMEM((36, KW, SUB), BF16),
            pltpu.VMEM((5, ROWS + HL, 128), F32),
            pltpu.VMEM((CAP, RB, QW), BF16),
            pltpu.VMEM((CAP, RB, QW), BF16),
            pltpu.VMEM((ROWS, 128), F32),
            pltpu.VMEM((ROWS + HL, 128), F32),
            pltpu.VMEM((4, ROWS + HL, 128), F32),
            pltpu.VMEM((CAP, RB, DV), BF16),
            pltpu.VMEM((CAP, RB, DV), BF16),
            pltpu.VMEM((HL * S, ROWS), BF16),
            dma((12,)), dma((2 * SLOTS,)), dma((2 * SLOTS,)), dma((36,)), dma((36,)),
            dma((2,)), dma((2,)), dma((SLOTS,)), dma((SLOTS,)),
        ],
        compiler_params=pltpu.CompilerParams(collective_id=0, has_side_effects=True, vmem_limit_bytes=56 << 20),
        cost_estimate=pl.CostEstimate(flops=16 << 30, bytes_accessed=8 << 20, transcendentals=8 << 20),
    )(
        jnp.swapaxes(latent_cache, 1, 2), query_nope, query_rope, new_latent, key_up, value_up,
        prompt_owner, prompt_length, sample_prompt.reshape(1, -1),
    )


def solution(mesh):
    return jax.shard_map(
        shards,
        mesh=mesh,
        in_specs=(
            P("rep", "tp", None),
            P("rep", "tp"),
            P("rep", "tp"),
            P("rep", None),
            P("tp", None, None),
            P("tp", None, None),
            P(),
            P(),
            P("rep", None),
        ),
        out_specs=P("rep", "tp"),
        check_vma=False,
    )
```

```python
import functools

import jax
import jax.numpy as jnp
from jax import lax
from jax.experimental import pallas as pl
from jax.experimental.pallas import tpu as pltpu
from jax.sharding import PartitionSpec as P

MESH = pl.DeviceIdType.MESH
NEG = -1e30
F32, BF16 = jnp.float32, jnp.bfloat16

S, HL, SLOTS, CAP = 24, 16, 16, 3
PL = SLOTS * CAP
ROWS = PL * HL
LAT, ROPE, NOPE, DV = 512, 64, 128, 128
QW = LAT + 2 * ROPE
SHARD, SUB = 1024, 256
KW = LAT + ROPE
RB = SLOTS * HL
NEAR_HEADS = 6
EARLY = 5


def dot(a, b):
    return jnp.dot(a, b, preferred_element_type=F32)


def dot_nt(a, b):
    return lax.dot_general(a, b, (((1,), (1,)), ((), ())), preferred_element_type=F32)


def swap(n, i):
    return sum((n // b % 2 + i // b % 2 - 2 * (n // b % 2) * (i // b % 2)) * b for b in (1, 2, 4, 8))


def block(i):
    return pl.ds(pl.multiple_of(i * HL, HL), HL)


def iota(shape, dim):
    return lax.broadcasted_iota(jnp.int32, shape, dim)


def kernel(
    latent, nope_h, rope_h, new_h, ku_h, vu_h, owner_h, length_h, labels_h, out,
    labels, owner, length, nope, rope, new, ku, vu, kv, stage, qsend, q, mtop, tot, acc, osend, orecv, unplace,
    lsem, qss, qrs, kss, krs, vss, vrs, oss, ors,
):
    r, t = lax.axis_index("rep"), lax.axis_index("tp")
    y, xh, c, z, xl = r // 4, (r // 2) % 2, r % 2, t // 2, t % 2
    role_a = c == xl

    def dev(yy, xx, zz, cc):
        return ((yy * 2 + xx // 2) * 2 + cc, zz * 2 + xx % 2)

    x = xh * 2 + xl
    zp, zm = dev(y, x, (z + 1) % 4, c), dev(y, x, (z + 3) % 4, c)
    sib = dev(y, x, z, 1 - c)
    partner = dev(y, xh * 2 + 1 - xl, z, 1 - c)
    slot = (y * 2 + xh) * 2 + xl

    barrier = pltpu.get_barrier_semaphore()

    def greet(d):
        pl.semaphore_signal(barrier, inc=1, device_id=d, device_id_type=MESH)

    hops = (0, 1, 2, 1)
    for i in sorted(range(16), key=lambda i: -hops[i // 4] - hops[i % 4]):
        yy, xx = (y + i // 4) % 4, (x + i % 4) % 4
        if i == 0:
            pl.when(jnp.logical_not(role_a))(functools.partial(greet, dev(y, x, z, xl)))
        else:
            greet(dev(yy, xx, z, xl))
        if i % 2 == 0:
            greet(dev(yy, (xx + xl + c) % 4, z, 1 - xl))
    for d in (zp, zm):
        greet(d)

    base = jnp.where(role_a, 0, 32)
    loads = [
        pltpu.make_async_copy(nope_h, nope, lsem.at[0]),
        pltpu.make_async_copy(rope_h, rope, lsem.at[1]),
        pltpu.make_async_copy(new_h, new, lsem.at[2]),
        pltpu.make_async_copy(ku_h, ku, lsem.at[3]),
        pltpu.make_async_copy(labels_h, labels, lsem.at[9]),
        pltpu.make_async_copy(owner_h, owner, lsem.at[10]),
        pltpu.make_async_copy(length_h, length, lsem.at[11]),
    ] + [pltpu.make_async_copy(latent.at[0, :, pl.ds(u * SUB, SUB)], kv.at[base + u], lsem.at[4 + u]) for u in range(4)]
    for load in loads:
        load.start()
    vload = pltpu.make_async_copy(vu_h, vu, lsem.at[8])
    pl.when(role_a)(vload.start)

    for load in loads[4:7]:
        load.wait()
    lab_row = labels[...]
    sub, lane = iota((S, S), 0), iota((S, S), 1)
    lab = jnp.sum(jnp.where(sub == lane, lab_row.astype(F32), 0.0), axis=1, keepdims=True).astype(jnp.int32)
    same = lab == lab_row
    rank_row = jnp.sum(jnp.where(same & (sub < lane), 1.0, 0.0), axis=0, keepdims=True).astype(jnp.int32)
    rank_col = jnp.sum(jnp.where(same & (lane < sub), 1.0, 0.0), axis=1, keepdims=True).astype(jnp.int32)
    slot_row, slot_col = jnp.zeros_like(lab_row), jnp.zeros_like(lab)
    live = jnp.int32(0)
    for p in range(SLOTS):
        own = owner[p]
        slot_row = jnp.where(lab_row == p, own, slot_row)
        slot_col = jnp.where(lab == p, own, slot_col)
        live = live + jnp.where(own == slot, length[p], 0)
    place = (iota((PL, S), 0) == rank_row * SLOTS + slot_row).astype(BF16)
    code = rank_col * SLOTS + slot_col

    for load in loads[:4] + loads[7:]:
        load.wait()
    scale = (NOPE + ROPE) ** -0.5
    nope_s = dot(place, nope[...]).astype(BF16)
    rope_s = dot(place, rope[...]) * scale
    new_s = dot(place, new[...])
    new_s = jnp.concatenate([new_s[:, :LAT], jnp.concatenate([new_s[:, LAT:], jnp.zeros((PL, ROPE), F32)], axis=1)], axis=1)
    low = iota((PL, 2 * ROPE), 1) < ROPE
    def absorb(h):
        rows = pl.ds(h, PL, stride=HL)
        lat_q = dot(nope_s[:, NOPE * h : NOPE * (h + 1)], ku[h]) * scale
        for j in range(4):
            stage[j, rows, :] = lat_q[:, 128 * j : 128 * j + 128]
        b = 128 * (h // 2)
        mine = rope_s[:, b : b + 128]
        if h % 2:
            mine = pltpu.roll(mine, ROPE, 1)
        if h < 9:
            piece = new_s[:, b : b + 128]
            if h % 2 == 0:
                piece = pltpu.roll(piece, ROPE, 1)
        else:
            piece = jnp.zeros_like(mine)
        stage[4, rows, :] = jnp.where(low, mine, piece)
    for h in range(HL // 4):
        absorb(h)

    places = (pl.ds(0, 1), pl.ds(1, 2))

    def q_copy(n, s, d):
        return pltpu.make_async_remote_copy(
            src_ref=qsend.at[places[n], block(s)], dst_ref=q.at[places[n], block(r)],
            send_sem=qss.at[n * SLOTS + s], recv_sem=qrs.at[n * SLOTS + r], device_id=d, device_id_type=MESH,
        )

    def q_dev(s):
        return dev(s // 4, ((s // 2) % 2) * 2 + s % 2, z, xl)

    def own_q(n):
        return pltpu.make_async_copy(qsend.at[places[n], block(r)], q.at[places[n], block(r)], qrs.at[n * SLOTS + r])

    def kv_copy(src, dst, sem, d):
        return pltpu.make_async_remote_copy(
            src_ref=kv.at[src], dst_ref=kv.at[dst], send_sem=kss.at[sem], recv_sem=krs.at[dst], device_id=d, device_id_type=MESH
        )

    def half_copy(src, dst, half, sem, d):
        lanes = pl.ds(half * (SUB // 2), SUB // 2)
        return pltpu.make_async_remote_copy(
            src_ref=kv.at[src, :, lanes], dst_ref=kv.at[dst, :, lanes], send_sem=kss.at[sem],
            recv_sem=krs.at[dst if half == 0 else 32 + dst // 16 * 2 + dst % 2], device_id=d, device_id_type=MESH,
        )

    o = jnp.where(role_a, 0, 16)

    def ring_own(u):
        return [kv_copy(o + u, o + 4 + u, u, zp), kv_copy(o + u, o + 8 + u, 4 + u, zm), kv_copy(o + u, o + u, 12 + u, sib)]

    def pair(j):
        if j < 2:
            return 2 * j, 2 * j + 1
        return (2 + j, 8 + (j - 2 ^ 1)) if j < 6 else (2 * j, 2 * j + 1)

    def ring_pass(j):
        a, b = pair(j)
        on_a, on_b = ([kv_copy(o + k, o + k, 12 + k, sib)] for k in (a, b))
        if j == 2:
            on_a = [kv_copy(o + a, o + 12, 8, zp)] + on_a
            on_b = [kv_copy(o + b, o + 13, 9, zm)] + on_b
        if j == 4:
            on_a = [half_copy(o + a, o + 14, n, 10 + 22 * n, zp) for n in range(2)] + on_a
            on_b = [half_copy(o + b, o + 15, n, 11 + 22 * n, zm) for n in range(2)] + on_b
        return on_a, on_b

    def last_pass(n):
        return [half_copy(o + 14, o + 14, n, 26 + 8 * n, sib), half_copy(o + 15, o + 15, n, 27 + 8 * n, sib)]

    def arrived(k):
        kv_copy(k, k, 0, sib).wait_recv()

    def half_arrived(k, n):
        half_copy(k, k, n, 0, sib).wait_recv()

    def ring_step(j):
        for k, onward in zip(pair(j), ring_pass(j)):
            arrived(o + k)
            for cp in onward:
                cp.start()

    def last_step(n):
        for k, cp in zip((14, 15), last_pass(n)):
            half_arrived(o + k, n)
            cp.start()

    def cross_step(u):
        arrived(16 + u)
        for cp in ring_own(u):
            cp.start()

    cross = [kv_copy(32 + u, 16 + u, 28 + u, partner) for u in range(4)]

    pl.semaphore_wait(barrier, jnp.where(role_a, 25, 26))

    @pl.when(role_a)
    def _():
        by_part = [ring_own(u) for u in range(4)]
        for u in range(4):
            by_part[u][0].start()
            by_part[u ^ 1][1].start()
            by_part[u][2].start()

    for h in range(HL // 4, HL):
        absorb(h)
    for j in range(5):
        qsend[:, :, pl.ds(128 * j, 128)] = stage[j, pl.ds(0, ROWS), :].astype(BF16).reshape(CAP, RB, 128)

    for n in range(2):
        for i in range(SLOTS):
            s = swap(slot, i)
            if i:
                q_copy(n, s, q_dev(s)).start()
            else:
                pl.when(role_a)(own_q(n).start)
                pl.when(jnp.logical_not(role_a))(q_copy(n, s, q_dev(s)).start)

    @pl.when(jnp.logical_not(role_a))
    def _():
        for cp in cross:
            cp.start()

    def q_wait(n, i, _):
        g = (r + i) % SLOTS
        kept = jnp.logical_and(role_a, i == 0)
        pl.when(kept)(lambda: own_q(n).wait())

        @pl.when(jnp.logical_not(kept))
        def _():
            pltpu.make_async_remote_copy(
                src_ref=qsend.at[places[n], block(0)], dst_ref=q.at[places[n], block(g)],
                send_sem=qss.at[0], recv_sem=qrs.at[n * SLOTS + g], device_id=sib, device_id_type=MESH,
            ).wait_recv()
        return 0

    def value_part(k, first, count):
        return pltpu.make_async_remote_copy(
            src_ref=vu_h.at[pl.ds(first, count)], dst_ref=vu.at[pl.ds(first, count)], send_sem=vss.at[k], recv_sem=vrs.at[k],
            device_id=dev(y, (xh if k == 0 else 1 - xh) * 2 + 1 - xl, z, c), device_id_type=MESH,
        )

    halves = [value_part(0, 0, NEAR_HEADS), value_part(1, NEAR_HEADS, HL - NEAR_HEADS)]

    wanted = jnp.concatenate([code * HL + h for h in range(HL)], axis=0)
    unplace[...] = (iota((HL * S, ROWS), 1) == wanted).astype(BF16)

    low_b = low[:SLOTS]
    wide_low = iota((RB, 2 * ROPE), 1) < ROPE
    by_row = (iota((RB, SLOTS), 0) // HL == iota((RB, SLOTS), 1)).astype(BF16)

    def open_block(b):
        rs = pl.ds(b * RB, RB)
        qb = q[b]
        tail = qb[:, LAT:].astype(F32)
        stage[0, rs, :] = tail
        pieces = [stage[0, pl.ds(b * RB + k, SLOTS, stride=HL), :] for k in range(9)]
        new_p = []
        for k in range(5):
            left = pltpu.roll(pieces[2 * k], ROPE, 1)
            new_p.append(jnp.where(low_b, left, pieces[2 * k + 1] if k < 4 else 0.0))
        own_keys = dot(by_row, jnp.concatenate(new_p, axis=1).astype(BF16))
        own_score = jnp.sum(qb[:, :LAT].astype(F32) * own_keys[:, :LAT], axis=1, keepdims=True)
        own_score = own_score + jnp.sum(jnp.where(wide_low, tail, 0.0) * own_keys[:, LAT:], axis=1, keepdims=True)
        for j in range(4):
            acc[j, rs, :] = own_keys[:, 128 * j : 128 * j + 128]
        mtop[rs, :] = jnp.broadcast_to(own_score, (RB, 128))
        tot[rs, :] = (iota((RB, 128), 1) == 0).astype(F32)

    def first(k):
        s = k % 16 // 4
        zz = (z + jnp.where(s == 1, 3, jnp.where(s == 2, 1, jnp.where(s == 3, 2, 0)))) % 4
        return (zz * 2 + jnp.where(k < 16, xl, 1 - xl)) * SHARD + k % 4 * SUB

    def attend(ka, kb, blocks, start=0, width=SUB):
        lanes = pl.ds(start, width)
        keys = jnp.concatenate([kv[ka, :, lanes], kv[kb, :, lanes]], axis=1)
        lane = iota((1, 2 * width), 1)
        at = lane + start + jnp.where(lane < width, first(ka), first(kb) - width)
        bias = jnp.where(at < live, 0.0, NEG)

        scores = [dot(q[b, :, pl.ds(0, KW)], keys) + bias for b in blocks]
        shrinks, weights_bf = [], []
        for b, s in zip(blocks, scores):
            rs = pl.ds(b * RB, RB)
            tiles = [s[:, 128 * j : 128 * j + 128] for j in range(2 * width // 128)]
            top = mtop[rs, :]
            new_top = jnp.maximum(top, jnp.max(functools.reduce(jnp.maximum, tiles), axis=1, keepdims=True))
            shrink = jnp.exp(top - new_top)
            weights = [jnp.exp(a - new_top) for a in tiles]
            tot[rs, :] = tot[rs, :] * shrink + functools.reduce(jnp.add, weights)
            mtop[rs, :] = new_top
            shrinks.append(shrink)
            weights_bf.append(jnp.concatenate([a.astype(BF16) for a in weights], axis=1))
        for b, shrink, w in zip(blocks, shrinks, weights_bf):
            rs = pl.ds(b * RB, RB)
            new = dot_nt(w, keys[:LAT])
            for j in range(4):
                acc[j, rs, :] = acc[j, rs, :] * shrink + new[:, 128 * j : 128 * j + 128]

    turns_a = {0: {2: 2, 3: 3, 4: 4}, 1: {1: 5, 4: 6}, 2: {}}
    turns_x = {0: {}, 1: {2: 0, 4: 1}, 2: {7: 2, 8: 3}}
    turns_b = {0: {}, 1: {}, 2: {9: 2, 10: 3, 12: 4, 13: 5, 14: 6}}

    def step(loop, blocks, i, _):
        j = i % 8
        inner = jnp.logical_and(j >= 2, j < 6)
        ka = jnp.where(inner, 2 + j, 2 * j) + i // 8 * 16
        kb = jnp.where(inner, 7 + j - j % 2 * 2, 2 * j + 1) + i // 8 * 16

        def both():
            arrived(ka)
            arrived(kb)

        @pl.when(role_a)
        def _():
            for at, k in turns_a[loop].items():
                pl.when(i == at)(functools.partial(ring_step, k))
            if loop == 2:

                @pl.when(i == 7)
                def _():
                    last_step(0)
                    last_step(1)

                pl.when(i == 5)(halves[1].start)
                pl.when(i == 8)(halves[0].start)
                pl.when(i >= 8)(both)

        @pl.when(jnp.logical_not(role_a))
        def _():
            for at, k in turns_x[loop].items():
                pl.when(i == at)(functools.partial(cross_step, k))
            for at, k in turns_b[loop].items():
                pl.when(i == at)(functools.partial(ring_step, k))
            if loop == 0:
                both()
            if loop == 2:
                pl.when(i < 7)(both)

                @pl.when(i == 7)
                def _():
                    for n in range(2):
                        half_arrived(14, n)
                        half_arrived(15, n)

        attend(ka, kb, blocks)
        return 0

    lax.fori_loop(0, SLOTS, functools.partial(q_wait, 0), 0)
    open_block(0)
    lax.fori_loop(0, EARLY, functools.partial(step, 0, (0,)), 0)
    lax.fori_loop(0, SLOTS, functools.partial(q_wait, 1), 0)
    open_block(1)
    open_block(2)
    lax.fori_loop(0, EARLY, functools.partial(step, 1, (1, 2)), 0)
    lax.fori_loop(EARLY, 15, functools.partial(step, 2, (0, 1, 2)), 0)
    for n in range(2):
        pl.when(jnp.logical_not(role_a))(functools.partial(last_step, n))

        @pl.when(role_a)
        def _():
            half_arrived(30, n)
            half_arrived(31, n)

        attend(30, 31, (0, 1, 2), n * (SUB // 2), SUB // 2)

    @pl.when(role_a)
    def _():
        vload.wait()

    @pl.when(jnp.logical_not(role_a))
    def _():
        for cp in halves:
            cp.wait_recv()

    for h in range(HL):
        rows = pl.ds(h, PL, stride=HL)
        share = 1.0 / jnp.sum(tot[rows, :], axis=1, keepdims=True)
        mean = jnp.concatenate([acc[j, rows, :] * share for j in range(4)], axis=1).astype(BF16)
        stage[0, rows, :] = dot(mean, vu[h])
    osend[...] = stage[0, pl.ds(0, ROWS), :].astype(BF16).reshape(CAP, RB, DV)

    def o_copy(g):
        return pltpu.make_async_remote_copy(
            src_ref=osend.at[:, block(g)], dst_ref=orecv.at[:, block(slot)], send_sem=oss.at[g], recv_sem=ors.at[slot],
            device_id=(g, z * 2 + c), device_id_type=MESH,
        )

    own_o = pltpu.make_async_copy(osend.at[:, block(r)], orecv.at[:, block(r)], ors.at[r])

    for iy in (2, 1, 3, 0):
        for ix, ic in ((1, 0), (1, 1), (0, 0), (0, 1)):
            g = ((y + iy) % 4 * 2 + (xh + ix) % 2) * 2 + (c + ic) % 2
            if iy + ix + ic:
                o_copy(g).start()
            else:
                pl.when(role_a)(own_o.start)
                pl.when(jnp.logical_not(role_a))(o_copy(g).start)

    @pl.when(role_a)
    def _():
        for cp in halves:
            cp.wait_send()

    @pl.when(jnp.logical_not(role_a))
    def _():
        for cp in cross:
            cp.wait_send()

    for u in range(4):
        for cp in ring_own(u):
            cp.wait_send()
    for j in range(2, 7):
        for onward in ring_pass(j):
            for cp in onward:
                cp.wait_send()
    for n in range(2):
        for cp in last_pass(n):
            cp.wait_send()

    def all_wait(i, _):
        s = (slot + i) % SLOTS
        g = (r + i) % SLOTS
        kept = jnp.logical_and(role_a, i == 0)

        @pl.when(kept)
        def _():
            own_o.wait()

        @pl.when(jnp.logical_not(kept))
        def _():
            q_copy(0, s, sib).wait_send()
            q_copy(1, s, sib).wait_send()
            o_copy(g).wait_send()
            pltpu.make_async_remote_copy(
                src_ref=osend.at[:, block(0)], dst_ref=orecv.at[:, block(s)], send_sem=oss.at[0], recv_sem=ors.at[s],
                device_id=sib, device_id_type=MESH,
            ).wait_recv()
        return 0

    lax.fori_loop(0, SLOTS, all_wait, 0)
    picked = dot(unplace[...], orecv[...].reshape(ROWS, DV))
    for h in range(HL):
        out[:, pl.ds(DV * h, DV)] = picked[S * h : S * (h + 1)].astype(BF16)


def shards(latent_cache, query_nope, query_rope, new_latent, key_up, value_up, prompt_owner, prompt_length, sample_prompt):
    hbm, vmem = (pl.BlockSpec(memory_space=m) for m in (pl.ANY, pltpu.VMEM))
    dma = pltpu.SemaphoreType.DMA
    return pl.pallas_call(
        kernel,
        out_shape=pltpu.VMEM(query_nope.shape, BF16),
        in_specs=[hbm] * 9,
        out_specs=vmem,
        scratch_shapes=[
            pltpu.VMEM((1, S), jnp.int32),
            pltpu.SMEM((SLOTS,), jnp.int32),
            pltpu.SMEM((SLOTS,), jnp.int32),
            pltpu.VMEM(query_nope.shape, BF16),
            pltpu.VMEM(query_rope.shape, BF16),
            pltpu.VMEM(new_latent.shape, BF16),
            pltpu.VMEM(key_up.shape, BF16),
            pltpu.VMEM(value_up.shape, BF16),
            pltpu.VMEM((36, KW, SUB), BF16),
            pltpu.VMEM((5, ROWS + HL, 128), F32),
            pltpu.VMEM((CAP, RB, QW), BF16),
            pltpu.VMEM((CAP, RB, QW), BF16),
            pltpu.VMEM((ROWS, 128), F32),
            pltpu.VMEM((ROWS + HL, 128), F32),
            pltpu.VMEM((4, ROWS + HL, 128), F32),
            pltpu.VMEM((CAP, RB, DV), BF16),
            pltpu.VMEM((CAP, RB, DV), BF16),
            pltpu.VMEM((HL * S, ROWS), BF16),
            dma((12,)), dma((2 * SLOTS,)), dma((2 * SLOTS,)), dma((36,)), dma((36,)),
            dma((2,)), dma((2,)), dma((SLOTS,)), dma((SLOTS,)),
        ],
        compiler_params=pltpu.CompilerParams(collective_id=0, has_side_effects=True, vmem_limit_bytes=56 << 20),
        cost_estimate=pl.CostEstimate(flops=16 << 30, bytes_accessed=8 << 20, transcendentals=8 << 20),
    )(
        jnp.swapaxes(latent_cache, 1, 2), query_nope, query_rope, new_latent, key_up, value_up,
        prompt_owner, prompt_length, sample_prompt.reshape(1, -1),
    )


def solution(mesh):
    return jax.shard_map(
        shards,
        mesh=mesh,
        in_specs=(
            P("rep", "tp", None),
            P("rep", "tp"),
            P("rep", "tp"),
            P("rep", None),
            P("tp", None, None),
            P("tp", None, None),
            P(),
            P(),
            P("rep", None),
        ),
        out_specs=P("rep", "tp"),
        check_vma=False,
    )
```
